128 devices in a mesh: shot: 2 (over y_hi), gx: 8 (over y_lo, z), gy: 8 (over x, core).
Axes of the slice: x: 4, y: 4 (y_hi: 2, y_lo: 2; y = y_hi * 2 + y_lo), z: 4, core: 2. Of those that a mesh axis runs over, the one named last changes fastest.
Arguments:
- coef: float32 [256, 256, 256], P('gx', 'gy'), may hold values from 0.1 to 0.3
- wave_now: float32 [2, 256, 256, 256], P('shot', 'gx', 'gy'), may hold values from -6 to 6
- wave_prev: float32 [2, 256, 256, 256], P('shot', 'gx', 'gy'), may hold values from -6 to 6
- adjoint_next: float32 [2, 256, 256, 256], P('shot', 'gx', 'gy'), may hold values from -1.5 to 1.5
- adjoint_after: float32 [2, 256, 256, 256], P('shot', 'gx', 'gy'), may hold values from -1.5 to 1.5
- noise: float32 [256, 256, 256], P('gx', 'gy'), may hold values from -6 to 6
- observed: float32 [2, 4096, 16], P('shot', ('gx', 'gy')), may hold values from -6 to 6
- recv_tile: int32 [4096, 1], P(('gx', 'gy')), may hold values from 0 to 63; in each aligned block of 64 rows (0 to 63, 64 to 127, ...) at most 2 rows name the same one
- recv_cell: int32 [4096], P(('gx', 'gy')), may hold values from 0 to 1023
Outputs:
- sample: float32 [256, 256, 256], P('gx', 'gy')
- gradient: float32 [256, 256, 256], P('gx', 'gy')
The draws below stay inside these ranges and needn't reach their ends.
Inputs may be any that keep to these rules, and one draw needn't show every extreme that they name: `recv_tile`: among the receivers of one device no tile appears more than 2 times, a bound that some block reaches; every tile holds some receiver.
All inputs are finite; a program needn't handle non-finite values.
Results may differ from the reference program's by a relative error of at most 0.00025.
Values sent between devices are 32-bit elements; how exact they have to be, the bound alone decides.
No kernel may reach another device: no remote copies, remote signals or barrier semaphores. Data moves between devices by JAX's collectives and lax.ppermute only.
A program may use at most 128 MiB of HBM per device.

```python
import math
import jax
import jax.numpy as jnp
import numpy as np
from jax import lax

CX = 32
CY = 32
NZ = 256
STEPS = 16
R_DEV = 64
CAP = 2
DEPTH = 2
NX = 256
NY = 256
RECV = 4096
SHOTS = 2
N_GX = 8
N_GY = 8


def place_ends(entries, rng, least, largest):
    spot = [jax.random.randint(jax.random.fold_in(rng, axis), (), 0, length) for axis, length in enumerate(entries.shape)]
    main_axis = entries.shape.index(max(entries.shape))
    next_to = spot[:main_axis] + [(spot[main_axis] + 1) % entries.shape[main_axis]] + spot[main_axis + 1:]
    return entries.at[tuple(spot)].set(least).at[tuple(next_to)].set(largest)


def steps_of(key, shape, split, low, high):
    gain, own = 1.0, jax.random.fold_in(key, 6)
    for axis_at, shards_of in split:
        steps = jnp.exp(jax.random.uniform(jax.random.fold_in(own, axis_at), (shards_of,), jnp.float32, low / len(split), high / len(split)))
        gain = gain * jnp.repeat(steps, shape[axis_at] // shards_of).reshape([-1 if axis == axis_at else 1 for axis in range(len(shape))])
    return gain


def assign_block(key, own, number, rows, number_of, top, most, lean):
    ranking = jax.random.permutation(key, number_of)
    crowded, ordinary = shares(number_of, rows * top, most, lean, True), shares(number_of, rows * top, most, lean, False)
    places = jnp.arange(number_of)

    def named(tallies, offset_by):
        used = int((tallies > 0).sum())
        fixed = max(1, used // 4)
        moved = fixed + (places - fixed + offset_by * (used - fixed)) % max(1, number_of - fixed)
        return jnp.zeros((number_of,), jnp.int32).at[ranking[jnp.where(places < fixed, places, moved)]].set(jnp.asarray(tallies, jnp.int32))

    tallies = jnp.where(number % 4 == 0, named(crowded, number // 4), named(ordinary, number - number // 4 - 1))
    mixed = jax.random.permutation(jax.random.fold_in(own, 3), number_of)
    source_of, sink = mixed[0:number_of // 2 * 2:2], mixed[1:number_of // 2 * 2:2]
    margin = jnp.minimum(tallies[source_of] - 1, most - tallies[sink]) // 2
    margin = jnp.where((source_of == ranking[0]) | (sink == ranking[0]) | (tallies[sink] == 0), 0, jnp.maximum(margin, 0))
    moved = jax.random.randint(jax.random.fold_in(own, 4), (number_of // 2,), 0, 1 << 20) % (margin + 1)
    tallies = tallies.at[source_of].add(-moved).at[sink].add(moved)
    labels = jnp.searchsorted(jnp.cumsum(tallies), jnp.arange(rows * top), side="right").astype(jnp.int32)
    table = labels.reshape(top, rows).T
    table = table[jax.random.permutation(jax.random.fold_in(own, 1), rows)]
    offset_by = jax.random.randint(jax.random.fold_in(own, 2), (rows, 1), 0, top)
    return jnp.take_along_axis(table, (jnp.arange(top)[None, :] + offset_by) % top, axis=1)


def shares(number_of, total, reach, lean, full):
    loads = [(1 << 20) // math.isqrt(grade ** lean) + 1 for grade in range(1, number_of + 1)]
    largest = reach if full else min(reach, max(-(-total // number_of), total * loads[0] // sum(loads)))
    least = 1 if total - largest >= number_of - 1 else 0
    holding, rest = [largest] + [least] * (number_of - 1), total - largest - least * (number_of - 1)
    while rest > 0:
        movable = [i for i in range(1, number_of) if holding[i] < largest] or [i for i in range(1, number_of) if holding[i] < reach]
        mass, budget = sum([loads[i] for i in movable]), rest
        for i in movable:
            addition = min(reach - holding[i], max(1, budget * loads[i] // mass), rest)
            holding[i] = holding[i] + addition
            rest = rest - addition
    return np.array(holding)


def gaussian(own_key, extent, spread, bound, shards=(), kind=jnp.bfloat16):
    entries = jax.random.normal(own_key, extent, jnp.float32) * spread
    if len(shards) > 0:
        entries = steps_of(own_key, extent, shards, -0.22, 0.18) * entries
    return jnp.clip(entries, min=-bound, max=bound).astype(kind)


def setup_inputs(seed: int = 0) -> dict:
    keys = jax.random.split(jax.random.key(seed), 10)
    coef = jnp.clip(0.1 + 0.20000001043081284 * jax.random.uniform(keys[0], (NX, NY, NZ), jnp.float32) ** steps_of(keys[0], (NX, NY, NZ), ((0, 8), (1, 8)), -0.2, 0.2), 0.1, 0.3)
    wave_now = gaussian(keys[1], (SHOTS, NX, NY, NZ), 1.0, 6.0, ((0, 2), (1, 8), (2, 8)), jnp.float32)
    wave_prev = gaussian(keys[2], (SHOTS, NX, NY, NZ), 1.0, 6.0, ((0, 2), (1, 8), (2, 8)), jnp.float32)
    adjoint_next = gaussian(keys[3], (SHOTS, NX, NY, NZ), 0.25, 1.5, ((0, 2), (1, 8), (2, 8)), jnp.float32)
    adjoint_after = gaussian(keys[4], (SHOTS, NX, NY, NZ), 0.25, 1.5, ((0, 2), (1, 8), (2, 8)), jnp.float32)
    noise = gaussian(keys[5], (NX, NY, NZ), 1.0, 6.0, ((0, 8), (1, 8)), jnp.float32)
    observed = gaussian(keys[6], (SHOTS, RECV, STEPS), 1.0, 6.0, ((0, 2), (1, 64)), jnp.float32)
    recv_tile_keys = jax.random.split(jax.random.fold_in(keys[7], 1), RECV // R_DEV)
    recv_tile_turns = jax.random.permutation(jax.random.fold_in(keys[7], 3), RECV // R_DEV)
    recv_tile = jax.vmap(lambda own, number: assign_block(jax.random.fold_in(keys[7], 2), own, number, R_DEV, N_GX * N_GY, 1, CAP, 2))(recv_tile_keys, recv_tile_turns).reshape((RECV, 1))
    recv_cell = place_ends(jax.random.randint(keys[8], (RECV,), 0, CX * CY), jax.random.fold_in(keys[8], 1), 0, (CX * CY) - 1).astype(jnp.int32)
    return {"coef": coef, "wave_now": wave_now, "wave_prev": wave_prev, "adjoint_next": adjoint_next, "adjoint_after": adjoint_after, "noise": noise, "observed": observed, "recv_tile": recv_tile, "recv_cell": recv_cell}


step_eta = 0.01
prior_prec = 4.0
prior_centre = 0.2

def lap_core(padded):
    centre = padded[1:-1, 1:-1]
    zero_face = jnp.zeros_like(centre[:, :, :1])
    shifted_up = jnp.concatenate((centre[:, :, 1:], zero_face), 2)
    shifted_down = jnp.concatenate((zero_face, centre[:, :, :-1]), 2)
    lateral = padded[2:, 1:-1] + padded[:-2, 1:-1] + padded[1:-1, 2:] + padded[1:-1, :-2]
    return lateral + shifted_up + shifted_down - 6.0 * centre

def pad_plane(field):
    return jnp.pad(field, ((1, 1), (1, 1), (0, 0)))

def reference(coef, wave_now, wave_prev, adjoint_next, adjoint_after, noise, observed, recv_tile, recv_cell):
    tile_of = recv_tile[:, 0]
    pos_x = tile_of // N_GY * CX + recv_cell // CY
    pos_y = tile_of % N_GY * CY + recv_cell % CY
    flat_cell = (pos_x * NY + pos_y).astype(jnp.int32)
    total = jnp.zeros(coef.shape, jnp.float32)
    for shot_index in range(SHOTS):

        def forward(carried, unused):
            previous, current = carried
            laplace = lap_core(pad_plane(current))
            updated = 2.0 * current - previous + coef * laplace
            return ((current, updated), (laplace, updated[:, :, DEPTH].reshape(-1)[flat_cell]))
        _, (laps, predicted) = lax.scan(forward, (wave_prev[shot_index], wave_now[shot_index]), None, length=STEPS)
        residual = predicted - observed[shot_index].T
        injected = jnp.zeros((STEPS, NX * NY), jnp.float32).at[:, flat_cell].add(residual)

        def backward(carried, inputs):
            later_one, later_two, gradient = carried
            laplace, inject_now = inputs
            adjoint = 2.0 * later_one - later_two + lap_core(pad_plane(coef * later_one))
            adjoint = adjoint.at[:, :, DEPTH].add(inject_now.reshape(NX, NY))
            return ((adjoint, later_one, gradient + laplace * adjoint), None)
        zeros_field = jnp.zeros(coef.shape, jnp.float32)
        start = (adjoint_next[shot_index], adjoint_after[shot_index], zeros_field)
        (_, _, gradient), _ = lax.scan(backward, start, (laps, injected), reverse=True)
        total = total + gradient
    sample = coef + step_eta * (prior_prec * (prior_centre - coef) - total) + math.sqrt(2.0 * step_eta) * noise
    return (sample, total)
```

```python
import functools
import math

import jax
import jax.numpy as jnp
from jax import lax
from jax.experimental import pallas as pl
from jax.experimental.pallas import tpu as pltpu
from jax.sharding import PartitionSpec as P

STEPS = 16
DEPTH = 2
K = 8
VMEM_LIMIT = 48 * 1024 * 1024

step_eta = 0.01
prior_prec = 4.0
prior_centre = 0.2


def pairs(count, odd):
    found = []
    for low in range(1 if odd else 0, count - 1, 2):
        found += [(low, low + 1), (low + 1, low)]
    return found


def swap(axis, even, low, high):
    count = lax.axis_size(axis)
    first = lax.ppermute(jnp.where(even, high, low), axis, pairs(count, False))
    second = lax.ppermute(jnp.where(even, low, high), axis, pairs(count, True))
    return first, second


def exchange(even_x, even_y, fields):
    rows, cols = fields.shape[1], fields.shape[2]
    x_first, x_second = swap("gx", even_x, fields[:, :K], fields[:, rows - K :])
    below = jnp.where(even_x, x_second, x_first)
    above = jnp.where(even_x, x_first, x_second)
    low = jnp.concatenate([below[:, :, :K], fields[:, :, :K], above[:, :, :K]], 1)
    high = jnp.concatenate(
        [below[:, :, cols - K :], fields[:, :, cols - K :], above[:, :, cols - K :]], 1
    )
    y_first, y_second = swap("gy", even_y, low, high)
    return x_first, x_second, y_first, y_second


def block_kernel(shape, adjoint, initial, base, parity, *refs):
    rows, cols, depth = shape
    own_refs, refs = refs[:3], refs[3:]
    halo_refs, refs = refs[:8], refs[8:]
    if adjoint:
        laps, inject, grad_in, newest, older, grad, first, second, coef, sems, out_sems = refs
    else:
        newest, older, laps, surface, first, second, coef, sems, out_sems = refs
    turn_of = pl.program_id(0)
    groups = cols // 8 + 2
    halves = depth // 128
    edge = K + 1
    lane = lax.broadcasted_iota(jnp.int32, (8, 128), 1)
    line = lax.broadcasted_iota(jnp.int32, (8, 128), 0)
    last_lane, first_lane = lane == 127, lane == 0
    last_line, first_line = line == 7, line == 0
    zero = jnp.zeros((8, 128), jnp.float32)

    @pl.when(turn_of == 0)
    def _():
        x_first = jnp.where(parity[0] == 0, rows + K, 0) + 1
        x_second = jnp.where(parity[0] == 0, 0, rows + K) + 1
        y_first = pl.multiple_of(jnp.where(parity[1] == 0, cols + K, 0), 8)
        y_second = pl.multiple_of(jnp.where(parity[1] == 0, 0, cols + K), 8)
        copies = []
        for index, (own, target) in enumerate(zip(own_refs, (first, second, coef))):
            halos = halo_refs[4:] if index == 2 else halo_refs[:4]
            inner = pl.ds(K, cols)
            for source, place in (
                (own, target.at[pl.ds(edge, rows), inner]),
                (halos[0].at[index], target.at[pl.ds(x_first, K), inner]),
                (halos[1].at[index], target.at[pl.ds(x_second, K), inner]),
                (halos[2].at[index], target.at[pl.ds(1, rows + 2 * K), pl.ds(y_first, K)]),
                (halos[3].at[index], target.at[pl.ds(1, rows + 2 * K), pl.ds(y_second, K)]),
            ):
                copies.append(pltpu.make_async_copy(source, place, sems.at[len(copies)]))
        for copy in copies:
            copy.start()
        for field in (first, second, coef):
            field[0] = jnp.zeros(field.shape[1:], jnp.float32)
            field[rows + 2 * K + 1] = jnp.zeros(field.shape[1:], jnp.float32)
        for copy in copies:
            copy.wait()
        if adjoint and initial:

            def weigh(x, carried):
                first[x] = first[x] * coef[x]
                second[x] = second[x] * coef[x]
                return carried

            lax.fori_loop(1, rows + 2 * K + 1, weigh, 0)
        if adjoint:
            grad[...] = grad_in[...]
        else:
            surface[...] = jnp.zeros(surface.shape, jnp.float32)

    def row(x, source, target, half, inside):
        step = 2 * turn_of + half
        if adjoint:
            turn = lax.rem(128 + DEPTH - (base - step), 128)
            slot = 1 - half
        else:
            turn = lax.rem(128 - DEPTH + base + step, 128)
            mark = lane == base + step
            slot = half

        def read(at_x, g, h):
            return source[at_x, pl.ds(8 * g, 8), pl.ds(128 * h, 128)]

        centre = [[read(x, g, h) for h in range(halves)] for g in range(groups)]
        ups = [[pltpu.roll(c, 7, 0) for c in line_of] for line_of in centre]
        downs = [[pltpu.roll(c, 1, 0) for c in line_of] for line_of in centre]
        done = []
        for g in range(groups):
            lefts = [pltpu.roll(c, 127, 1) for c in centre[g]]
            rights = [pltpu.roll(c, 1, 1) for c in centre[g]]
            for h in range(halves):
                c = centre[g][h]
                at = (x, pl.ds(8 * g, 8), pl.ds(128 * h, 128))
                up = jnp.where(last_line, ups[g + 1][h], ups[g][h]) if g + 1 < groups else ups[g][h]
                down = jnp.where(first_line, downs[g - 1][h], downs[g][h]) if g > 0 else downs[g][h]
                left = jnp.where(last_lane, lefts[h + 1] if h + 1 < halves else zero, lefts[h])
                right = jnp.where(first_lane, rights[h - 1] if h > 0 else zero, rights[h])
                lateral = (read(x + 1, g, h) + read(x - 1, g, h)) + (up + down)
                laplace = lateral + (left + right) - 6.0 * c
                forced = laplace
                if adjoint and h == 0:
                    moved = pltpu.roll(inject[x - 1, pl.ds(8 * g, 8), :], turn, 1)
                    forced = laplace + jnp.where(lane == DEPTH, moved, 0.0)
                fresh = (2.0 * c - target[at]) + coef[at] * forced
                done.append((g, h, at, laplace, fresh))
        for g, h, at, laplace, fresh in done:
            target[at] = fresh
            if inside and 0 < g < groups - 1:
                mine = (x - edge, pl.ds(8 * g - 8, 8), pl.ds(128 * h, 128))
                if adjoint:
                    grad[mine] = grad[mine] + laps[(slot,) + mine] * fresh
                else:
                    laps[(slot,) + mine] = laplace
                    if h == 0:
                        seen = pltpu.roll(fresh, turn, 1)
                        flat = (x - edge, pl.ds(8 * g - 8, 8), slice(None))
                        surface[flat] = jnp.where(mark, seen, surface[flat])

    def sweep(source, target, half):
        def rows_from(begin, count, unroll, inside):
            def body(index, carried):
                for offset in range(unroll):
                    row(begin + index * unroll + offset, source, target, half, inside)
                return carried

            lax.fori_loop(0, count, body, 0)

        count = K // 2 - turn_of - half
        rows_from(edge - 2 * count, count, 2, False)
        rows_from(edge, rows // 4, 4, True)
        rows_from(edge + rows, count, 2, False)

    sweep(first, second, 0)
    sweep(second, first, 1)

    @pl.when(turn_of == K // 2 - 1)
    def _():
        inner = (pl.ds(edge, rows), pl.ds(K, cols))
        out_new = pltpu.make_async_copy(first.at[inner], newest, out_sems.at[0])
        out_old = pltpu.make_async_copy(second.at[inner], older, out_sems.at[1])
        out_new.start()
        out_old.start()
        out_new.wait()
        out_old.wait()


def run_block(parity, current, previous, coef, halos, coef_halos, adjoint=None, base=0):
    rows, cols, depth = coef.shape
    extended = (rows + 2 * K + 2, cols + 2 * K)
    any_spec = pl.BlockSpec(memory_space=pl.ANY)
    field = jax.ShapeDtypeStruct(coef.shape, jnp.float32)
    whole = lambda shape: pl.BlockSpec(shape, lambda step: (0,) * len(shape))
    in_specs = [pl.BlockSpec(memory_space=pltpu.SMEM)] + [any_spec] * 11
    operands = [parity, current, previous, coef, *halos, *coef_halos]
    if adjoint is None:
        out_shape = [
            field,
            field,
            jax.ShapeDtypeStruct((K,) + coef.shape, jnp.float32),
            jax.ShapeDtypeStruct((rows, cols, 128), jnp.float32),
        ]
        out_specs = [
            any_spec,
            any_spec,
            pl.BlockSpec((2,) + coef.shape, lambda step: (step, 0, 0, 0)),
            whole((rows, cols, 128)),
        ]
        initial = False
    else:
        laps, inject, gradient, initial = adjoint
        operands += [laps, inject, gradient]
        in_specs += [
            pl.BlockSpec((2,) + coef.shape, lambda step: (K // 2 - 1 - step, 0, 0, 0)),
            whole(inject.shape),
            whole(coef.shape),
        ]
        out_shape = [field, field, field]
        out_specs = [any_spec, any_spec, whole(coef.shape)]
    return pl.pallas_call(
        functools.partial(block_kernel, coef.shape, adjoint is not None, initial, base),
        grid=(K // 2,),
        in_specs=in_specs,
        out_specs=out_specs,
        out_shape=out_shape,
        scratch_shapes=[
            pltpu.VMEM(extended + (depth,), jnp.float32),
            pltpu.VMEM(extended + (depth,), jnp.float32),
            pltpu.VMEM(extended + (depth,), jnp.float32),
            pltpu.SemaphoreType.DMA((15,)),
            pltpu.SemaphoreType.DMA((2,)),
        ],
        compiler_params=pltpu.CompilerParams(vmem_limit_bytes=VMEM_LIMIT),
    )(*operands)


def receivers(observed, recv_tile, recv_cell, cell_count):
    tile_count = lax.axis_size(("gx", "gy"))
    highest = lax.Precision.HIGHEST
    tile_of = recv_tile[:, 0]
    per_tile = max(2, 2 * observed.shape[1] // tile_count)
    slot_count = tile_count * per_tile
    owner_hot = (tile_of[:, None] == jnp.arange(tile_count, dtype=jnp.int32)[None, :]).astype(
        jnp.int32
    )
    before = jnp.cumsum(owner_hot, 0) - owner_hot
    slot_of = tile_of * per_tile + jnp.sum(before * owner_hot, 1)
    routing = (slot_of[None, :] == jnp.arange(slot_count, dtype=jnp.int32)[:, None]).astype(
        jnp.float32
    )
    marks = (recv_cell + 1).astype(jnp.float32)[:, None]
    outgoing = jnp.dot(
        routing,
        jnp.concatenate([observed[0], marks], 1),
        precision=highest,
        preferred_element_type=jnp.float32,
    )
    arrived = lax.all_to_all(
        outgoing.reshape(tile_count, per_tile, STEPS + 1),
        ("gx", "gy"),
        split_axis=0,
        concat_axis=0,
        tiled=True,
    ).reshape(slot_count, STEPS + 1)
    cells = arrived[:, STEPS].astype(jnp.int32) - 1
    picker = (jnp.arange(cell_count, dtype=jnp.int32)[:, None] == cells[None, :]).astype(
        jnp.float32
    )
    seen = jnp.dot(
        picker, arrived[:, :STEPS], precision=highest, preferred_element_type=jnp.float32
    )
    return jnp.sum(picker, 1, keepdims=True), seen


def local(
    coef, wave_now, wave_prev, adjoint_next, adjoint_after, noise, observed, recv_tile, recv_cell
):
    rows, cols, depth = coef.shape
    odd_x, odd_y = lax.axis_index("gx") % 2, lax.axis_index("gy") % 2
    parity = jnp.stack([odd_x, odd_y]).astype(jnp.int32)
    even = (odd_x == 0, odd_y == 0)
    trade = functools.partial(exchange, *even)

    wave_halos = trade(jnp.stack([wave_now[0], wave_prev[0], coef]))
    coef_halos = wave_halos
    adjoint_halos = trade(jnp.stack([adjoint_next[0], adjoint_after[0]]))
    counts, seen = receivers(observed, recv_tile, recv_cell, rows * cols)

    now, then, laps_early, surface_early = run_block(
        parity, wave_now[0], wave_prev[0], coef, wave_halos, coef_halos, base=0
    )
    _, _, laps_late, surface_late = run_block(
        parity, now, then, coef, trade(jnp.stack([now, then])), coef_halos, base=K
    )
    surface = (surface_early + surface_late)[:, :, :STEPS].reshape(rows * cols, STEPS)
    inject = (counts * surface - seen).reshape(1, rows, cols, STEPS)
    x_first, x_second, y_first, y_second = trade(inject)
    below, above = jnp.where(even[0], x_second, x_first), jnp.where(even[0], x_first, x_second)
    left, right = jnp.where(even[1], y_second, y_first), jnp.where(even[1], y_first, y_second)
    middle = jnp.concatenate([below[0], inject[0], above[0]], 0)
    inject = jnp.concatenate([left[0], middle, right[0]], 1)
    inject = jnp.pad(inject, ((0, 0), (0, 0), (0, 128 - STEPS)))

    now, then, gradient = run_block(
        parity,
        adjoint_next[0],
        adjoint_after[0],
        coef,
        adjoint_halos,
        coef_halos,
        adjoint=(laps_late, inject, jnp.zeros(coef.shape, jnp.float32), True),
        base=STEPS - 1,
    )
    _, _, gradient = run_block(
        parity,
        now,
        then,
        coef,
        trade(jnp.stack([now, then])),
        coef_halos,
        adjoint=(laps_early, inject, gradient, False),
        base=K - 1,
    )
    other = lax.ppermute(gradient, "shot", pairs(lax.axis_size("shot"), False))
    total = (gradient + other) / coef
    sample = (
        coef
        + step_eta * (prior_prec * (prior_centre - coef) - total)
        + math.sqrt(2.0 * step_eta) * noise
    )
    return (sample, total)


def solution(mesh):
    return jax.shard_map(
        local,
        mesh=mesh,
        in_specs=(
            P("gx", "gy", None),
            P("shot", "gx", "gy", None),
            P("shot", "gx", "gy", None),
            P("shot", "gx", "gy", None),
            P("shot", "gx", "gy", None),
            P("gx", "gy", None),
            P("shot", ("gx", "gy"), None),
            P(("gx", "gy"), None),
            P(("gx", "gy")),
        ),
        out_specs=(P("gx", "gy", None), P("gx", "gy", None)),
        check_vma=False,
    )
```

```python
import functools
import math

import jax
import jax.numpy as jnp
from jax import lax
from jax.experimental import pallas as pl
from jax.experimental.pallas import tpu as pltpu
from jax.sharding import PartitionSpec as P

STEPS = 16
DEPTH = 2
K = 8
UNROLL = 8
THIN = 32
MARK = 64
THIN_UNROLL = 4
VMEM_LIMIT = 48 * 1024 * 1024
STRIP_VMEM_LIMIT = 16 * 1024 * 1024

step_eta = 0.01
prior_prec = 4.0
prior_centre = 0.2


def pairs(count, odd):
    found = []
    for low in range(1 if odd else 0, count - 1, 2):
        found += [(low, low + 1), (low + 1, low)]
    return found


def swap(axis, first, second):
    count = lax.axis_size(axis)
    return (
        lax.ppermute(first, axis, pairs(count, False)),
        lax.ppermute(second, axis, pairs(count, True)),
    )


def strip_kernel(axis, width, count, parity, *refs):
    fields, refs = refs[:count], refs[count:]
    received, refs = refs[: 2 * axis], refs[2 * axis :]
    sends, sems = refs[:2], refs[2]
    rows, cols = fields[0].shape[:2]
    far = (rows, cols)[axis] - width
    even = parity[axis] == 0
    copies = []

    def copy(source, target):
        copies.append(pltpu.make_async_copy(source, target, sems.at[len(copies)]))

    for send, start in zip(sends, (jnp.where(even, far, 0), jnp.where(even, 0, far))):
        if axis == 1:
            part = pl.ds(pl.multiple_of(start, 8), width)
            above, below = rows + width, 0
            places = [jnp.where(parity[0] == 0, *pair) for pair in ((above, below), (below, above))]
        for index, field in enumerate(fields):
            if axis == 0:
                copy(field.at[pl.ds(start, width)], send.at[index])
            else:
                copy(field.at[:, part], send.at[index, pl.ds(width, rows)])
                for strip, place in zip(received, places):
                    copy(strip.at[index, :, part], send.at[index, pl.ds(place, width)])
    run_copies(copies)


def strips(parity, fields, axis, width, received=()):
    rows, cols, depth = fields[0].shape
    count = len(fields)
    shape = (count, width, cols, depth) if axis == 0 else (count, rows + 2 * width, width, depth)
    send = jax.ShapeDtypeStruct(shape, jnp.float32)
    anywhere = pl.BlockSpec(memory_space=pl.ANY)
    return pl.pallas_call(
        functools.partial(strip_kernel, axis, width, count),
        in_specs=[pl.BlockSpec(memory_space=pltpu.SMEM)] + [anywhere] * (count + len(received)),
        out_specs=[anywhere, anywhere],
        out_shape=[send, send],
        scratch_shapes=[pltpu.SemaphoreType.DMA(((2 + 4 * axis) * count,))],
        compiler_params=pltpu.CompilerParams(vmem_limit_bytes=STRIP_VMEM_LIMIT),
    )(parity, *fields, *received)


def halo_places(parity, shape, width, pad):
    rows, cols = shape[:2]
    x_first = jnp.where(parity[0] == 0, rows + width, 0) + pad
    x_second = jnp.where(parity[0] == 0, 0, rows + width) + pad
    y_first = pl.multiple_of(jnp.where(parity[1] == 0, cols + width, 0), 8)
    y_second = pl.multiple_of(jnp.where(parity[1] == 0, 0, cols + width), 8)
    inner, every = pl.ds(width, cols), pl.ds(pad, rows + 2 * width)
    return (
        (pl.ds(width + pad, rows), inner),
        (pl.ds(x_first, width), inner),
        (pl.ds(x_second, width), inner),
        (every, pl.ds(y_first, width)),
        (every, pl.ds(y_second, width)),
    )


def run_copies(copies, between=None):
    for copy in copies:
        copy.start()
    if between is not None:
        between()
    for copy in copies:
        copy.wait()


def block_kernel(shape, adjoint, gather, parity, *refs):
    rows, cols, depth = shape
    own_refs, refs = refs[:3], refs[3:]
    halo_refs, refs = refs[:8], refs[8:]
    if gather:
        factor, grad_in, refs = refs[0], refs[1], refs[2:]
    if gather and not adjoint:
        surface_in, refs = refs[0], refs[1:]
    if gather:
        grad, refs = refs[0], refs[1:]
    else:
        newest, older, send_first, send_second, kept = refs[:5]
        refs = refs[5:]
    if gather and not adjoint:
        kept, refs = refs[0], refs[1:]
    if not adjoint:
        surface, refs = refs[0], refs[1:]
    first, second, coef, sems, out_sems = refs
    turn_of = pl.program_id(0)
    groups = cols // 8 + 2
    halves = depth // 128
    edge = K + 1
    lane = lax.broadcasted_iota(jnp.int32, (8, 128), 1)
    line = lax.broadcasted_iota(jnp.int32, (8, 128), 0)
    last_lane, first_lane = lane == 127, lane == 0
    last_line, first_line = line == 7, line == 0
    zero = jnp.zeros((8, 128), jnp.float32)

    @pl.when(turn_of == 0)
    def _():
        places = halo_places(parity, shape, K, 1)
        copies = []
        for index, (own, target) in enumerate(zip(own_refs, (first, second, coef))):
            halos = halo_refs[4:] if index == 2 else halo_refs[:4]
            sources = [own] + [halo.at[index] for halo in halos]
            for source, place in zip(sources, places):
                copies.append(
                    pltpu.make_async_copy(source, target.at[place], sems.at[len(copies)])
                )

        def pads():
            for field in (first, second, coef):
                field[0] = jnp.zeros(field.shape[1:], jnp.float32)
                field[rows + 2 * K + 1] = jnp.zeros(field.shape[1:], jnp.float32)
            if gather:
                grad[...] = grad_in[...]
            if not adjoint:
                surface[...] = surface_in[...] if gather else jnp.zeros_like(surface)

        run_copies(copies, pads)
        if adjoint and not gather:

            def weigh(x, carried):
                first[x] = first[x] * coef[x]
                second[x] = second[x] * coef[x]
                return carried

            lax.fori_loop(1, rows + 2 * K + 1, weigh, 0)

    def load(source, x):
        return [
            [source[x, pl.ds(8 * g, 8), pl.ds(128 * h, 128)] for h in range(halves)]
            for g in range(groups)
        ]

    def row(x, target, half, inside, below, centre, above):
        ups = [[pltpu.roll(c, 7, 0) for c in line_of] for line_of in centre]
        downs = [[pltpu.roll(c, 1, 0) for c in line_of] for line_of in centre]
        done = []
        for g in range(groups):
            lefts = [pltpu.roll(c, 127, 1) for c in centre[g]]
            rights = [pltpu.roll(c, 1, 1) for c in centre[g]]
            for h in range(halves):
                c = centre[g][h]
                at = (x, pl.ds(8 * g, 8), pl.ds(128 * h, 128))
                up = jnp.where(last_line, ups[g + 1][h], ups[g][h]) if g + 1 < groups else ups[g][h]
                down = jnp.where(first_line, downs[g - 1][h], downs[g][h]) if g > 0 else downs[g][h]
                left = jnp.where(last_lane, lefts[h + 1] if h + 1 < halves else zero, lefts[h])
                right = jnp.where(first_lane, rights[h - 1] if h > 0 else zero, rights[h])
                lateral = (above[g][h] + below[g][h]) + (up + down)
                laplace = lateral + (left + right) - 6.0 * c
                fresh = (2.0 * c - target[at]) + coef[at] * laplace
                done.append((g, h, at, laplace, fresh))
        for g, h, at, laplace, fresh in done:
            target[at] = fresh
            if inside and 0 < g < groups - 1:
                mine = (x - edge, pl.ds(8 * g - 8, 8), pl.ds(128 * h, 128))
                term = fresh if adjoint else laplace
                if gather:
                    grad[mine] = grad[mine] + factor[(1 - half,) + mine] * term
                if not gather or (not adjoint and h == 0):
                    kept[(half,) + mine] = term
                if not adjoint and h == 0:
                    surface[mine] = jnp.where(lane == DEPTH, fresh, pltpu.roll(surface[mine], 1, 1))

    def sweep(source, target, half):
        def rows_from(begin, count, unroll, inside):
            def body(index, carried):
                below, centre = carried
                for offset in range(unroll):
                    x = begin + index * unroll + offset
                    above = load(source, x + 1)
                    row(x, target, half, inside, below, centre, above)
                    below, centre = centre, above
                return below, centre

            lax.fori_loop(0, count, body, (load(source, begin - 1), load(source, begin)))

        count = K // 2 - turn_of - half
        rows_from(edge - 2 * count, count, 2, False)
        rows_from(edge, rows // UNROLL, UNROLL, True)
        rows_from(edge + rows, count, 2, False)

    sweep(first, second, 0)
    sweep(second, first, 1)

    if not gather:

        @pl.when(turn_of == K // 2 - 1)
        def _():
            inner = pl.ds(K, cols)
            low, high = edge, edge + rows - K
            copies = []
            for index, (field, out) in enumerate(((first, newest), (second, older))):
                for source, target in (
                    (pl.ds(edge, rows), out),
                    (pl.ds(jnp.where(parity[0] == 0, high, low), K), send_first.at[index]),
                    (pl.ds(jnp.where(parity[0] == 0, low, high), K), send_second.at[index]),
                ):
                    copies.append(
                        pltpu.make_async_copy(
                            field.at[source, inner], target, out_sems.at[len(copies)]
                        )
                    )
            run_copies(copies)


def whole(shape):
    return pl.BlockSpec(shape, lambda step: (0,) * len(shape))


def run_block(parity, current, previous, coef, halos, coef_halos, adjoint, gather=None):
    rows, cols, depth = coef.shape
    extended = (rows + 2 * K + 2, cols + 2 * K, depth)
    any_spec = pl.BlockSpec(memory_space=pltpu.HBM)
    field = jax.ShapeDtypeStruct(coef.shape, jnp.float32)
    strips = jax.ShapeDtypeStruct((2, K, cols, depth), jnp.float32)
    flat = (rows, cols, 128)
    in_specs = [pl.BlockSpec(memory_space=pltpu.SMEM)] + [any_spec] * 11
    operands = [parity, current, previous, coef, *halos, *coef_halos]
    if gather is not None:
        operands += gather
        in_specs += [
            pl.BlockSpec((2,) + coef.shape, lambda step: (K // 2 - 1 - step, 0, 0, 0)),
            whole(coef.shape),
        ]
        if not adjoint:
            in_specs += [whole(flat)]
        out_shape, out_specs = [field], [whole(coef.shape)]
    else:
        out_shape = [field, field, strips, strips]
        out_specs = [any_spec] * 4
    if gather is None or not adjoint:
        kept = flat if gather is not None else coef.shape
        out_shape += [jax.ShapeDtypeStruct((K,) + kept, jnp.float32)]
        out_specs += [pl.BlockSpec((2,) + kept, lambda step: (step, 0, 0, 0))]
    if not adjoint:
        out_shape += [jax.ShapeDtypeStruct(flat, jnp.float32)]
        out_specs += [whole(flat)]
    return pl.pallas_call(
        functools.partial(block_kernel, coef.shape, adjoint, gather is not None),
        grid=(K // 2,),
        in_specs=in_specs,
        out_specs=out_specs,
        out_shape=out_shape,
        scratch_shapes=[pltpu.VMEM(extended, jnp.float32)] * 3
        + [pltpu.SemaphoreType.DMA((15,)), pltpu.SemaphoreType.DMA((6,))],
        cost_estimate=pl.CostEstimate(flops=10**8, bytes_accessed=6 * 10**7, transcendentals=0),
        compiler_params=pltpu.CompilerParams(vmem_limit_bytes=VMEM_LIMIT),
    )(*operands)


def thin_kernel(shape, parity, own, *refs):
    halo_refs, refs = refs[:4], refs[4:]
    laps_early, laps_late, packed_out, tile, first, second, coef, inject, grad, sems = refs
    rows, cols = shape[:2]
    turn_of = pl.program_id(0)
    blocks = 128 // THIN
    span = (rows + 2 * STEPS) // blocks
    groups = (cols + 2 * STEPS) // 8
    margin = STEPS // 8
    lane = lax.broadcasted_iota(jnp.int32, (8, 128), 1)
    line = lax.broadcasted_iota(jnp.int32, (8, 128), 0)
    in_block = lane % THIN
    last_lane, first_lane = in_block == THIN - 1, in_block == 0
    last_line, first_line = line == 7, line == 0

    def rows8(g):
        return pl.ds(8 * g, 8)

    @pl.when(turn_of == 0)
    def _():
        places = halo_places(parity, shape, STEPS, 0)
        sources = [own] + [halo.at[0] for halo in halo_refs]
        run_copies(
            [
                pltpu.make_async_copy(source, tile.at[place], sems.at[index])
                for index, (source, place) in enumerate(zip(sources, places))
            ]
        )
        first[...] = jnp.zeros_like(first)
        second[...] = jnp.zeros_like(second)
        grad[...] = jnp.zeros_like(grad)

        def pack(i, carried):
            for g in range(groups):
                forces, speeds = jnp.zeros((8, 128), jnp.float32), jnp.zeros((8, 128), jnp.float32)
                for block in range(blocks):
                    value = tile[block * span + i, rows8(g), :]
                    here = lane // THIN == block
                    forces = jnp.where(here, pltpu.roll(value, THIN * block, 1), forces)
                    speeds = jnp.where(
                        here, pltpu.roll(value, (THIN * block - THIN) % 128, 1), speeds
                    )
                inject[i, rows8(g), :] = forces
                coef[i, rows8(g), :] = speeds
            return carried

        lax.fori_loop(0, span, pack, 0)

    def sweep(source, target, half, laps):
        def load(i):
            return [source[i, rows8(g), :] for g in range(groups)]

        def body(index, carried):
            below, centre = carried
            for offset in range(THIN_UNROLL):
                i = index * THIN_UNROLL + offset
                above = load(i + 2)
                ups = [pltpu.roll(c, 7, 0) for c in centre]
                downs = [pltpu.roll(c, 1, 0) for c in centre]
                done = []
                for g, c in enumerate(centre):
                    up = jnp.where(last_line, ups[g + 1], ups[g]) if g + 1 < groups else ups[g]
                    down = jnp.where(first_line, downs[g - 1], downs[g]) if g > 0 else downs[g]
                    left = jnp.where(last_lane, 0.0, pltpu.roll(c, 127, 1))
                    right = jnp.where(first_lane, 0.0, pltpu.roll(c, 1, 1))
                    laplace = (above[g] + below[g]) + (up + down) + (left + right) - 6.0 * c
                    force = inject[i, rows8(g), :]
                    forced = laplace + jnp.where(in_block == DEPTH, force, 0.0)
                    fresh = (2.0 * c - target[i + 1, rows8(g), :]) + coef[i, rows8(g), :] * forced
                    done.append((g, pltpu.roll(force, 127, 1), fresh))
                for g, force, fresh in done:
                    inject[i, rows8(g), :] = force
                    target[i + 1, rows8(g), :] = fresh
                for g, _, fresh in done[margin : groups - margin]:
                    for block in range(rows // span):
                        moved = pltpu.roll(fresh, 128 - THIN * (block + STEPS // span), 1)
                        at = (block * span + i, rows8(g - margin), slice(None))
                        grad[at] = grad[at] + laps[(1 - half,) + at] * moved
                below, centre = centre, above
            return below, centre

        lax.fori_loop(0, span // THIN_UNROLL, body, (load(0), load(1)))
        for g in range(groups):
            target[0, rows8(g), :] = pltpu.roll(target[span, rows8(g), :], THIN, 1)
            target[span + 1, rows8(g), :] = pltpu.roll(target[1, rows8(g), :], 128 - THIN, 1)

    @pl.when(turn_of < STEPS // 4)
    def _():
        sweep(first, second, 0, laps_late)
        sweep(second, first, 1, laps_late)

    @pl.when(turn_of >= STEPS // 4)
    def _():
        sweep(first, second, 0, laps_early)
        sweep(second, first, 1, laps_early)

    @pl.when(turn_of == STEPS // 2 - 1)
    def _():
        height = rows // blocks
        for p in range(height):
            for g in range(cols // 8):
                value = jnp.zeros((8, 128), jnp.float32)
                for block in range(blocks):
                    moved = pltpu.roll(grad[block * height + p, rows8(g), :], THIN * block, 1)
                    value = jnp.where(lane // THIN == block, moved, value)
                packed_out[p, rows8(g), :] = value


def run_thin(parity, own, halos, laps_early, laps_late):
    rows, cols = own.shape[:2]
    extended = (rows + 2 * STEPS, cols + 2 * STEPS, 128)
    span = extended[0] * THIN // 128
    packed = (rows * THIN // 128, cols, 128)
    half = STEPS // 4
    any_spec = pl.BlockSpec(memory_space=pltpu.HBM)
    return pl.pallas_call(
        functools.partial(thin_kernel, own.shape),
        grid=(STEPS // 2,),
        in_specs=[pl.BlockSpec(memory_space=pltpu.SMEM)]
        + [any_spec] * 5
        + [
            pl.BlockSpec(
                (2, rows, cols, 128), lambda step: (jnp.minimum(half - 1, 2 * half - 1 - step), 0, 0, 0)
            ),
            pl.BlockSpec(
                (2, rows, cols, 128), lambda step: (jnp.maximum(0, half - 1 - step), 0, 0, 0)
            ),
        ],
        out_specs=whole(packed),
        out_shape=jax.ShapeDtypeStruct(packed, jnp.float32),
        scratch_shapes=[
            pltpu.VMEM(extended, jnp.float32),
            pltpu.VMEM((span + 2, extended[1], 128), jnp.float32),
            pltpu.VMEM((span + 2, extended[1], 128), jnp.float32),
            pltpu.VMEM((span, extended[1], 128), jnp.float32),
            pltpu.VMEM((span, extended[1], 128), jnp.float32),
            pltpu.VMEM((rows, cols, 128), jnp.float32),
            pltpu.SemaphoreType.DMA((5,)),
        ],
        cost_estimate=pl.CostEstimate(flops=10**8, bytes_accessed=5 * 10**7, transcendentals=0),
        compiler_params=pltpu.CompilerParams(vmem_limit_bytes=VMEM_LIMIT),
    )(parity, own, *halos, laps_early, laps_late)


def final_kernel(ours, theirs, thin_ours, thin_theirs, coef, noise, sample, total):
    block = pl.program_id(0)
    lane = lax.broadcasted_iota(jnp.int32, (8, 128), 1)
    for p in range(coef.shape[0]):
        for g in range(coef.shape[1] // 8):
            lines = pl.ds(8 * g, 8)
            thin = thin_ours[p, lines, :] + thin_theirs[p, lines, :]
            thin = jnp.where(lane < THIN, pltpu.roll(thin, lax.rem(128 - THIN * block, 128), 1), 0.0)
            for h in range(coef.shape[2] // 128):
                at = (p, lines, pl.ds(128 * h, 128))
                summed = ours[at] + theirs[at]
                if h == 0:
                    summed = summed + thin
                speed = coef[at]
                gradient = summed / speed
                total[at] = gradient
                sample[at] = (
                    speed
                    + step_eta * (prior_prec * (prior_centre - speed) - gradient)
                    + math.sqrt(2.0 * step_eta) * noise[at]
                )


def run_final(ours, theirs, thin_ours, thin_theirs, coef, noise):
    blocks = 128 // THIN
    part = pl.BlockSpec((coef.shape[0] // blocks,) + coef.shape[1:], lambda step: (step, 0, 0))
    thin = whole(thin_ours.shape)
    field = jax.ShapeDtypeStruct(coef.shape, jnp.float32)
    return pl.pallas_call(
        final_kernel,
        grid=(blocks,),
        in_specs=[part, part, thin, thin, part, part],
        out_specs=[part, part],
        out_shape=[field, field],
        compiler_params=pltpu.CompilerParams(vmem_limit_bytes=VMEM_LIMIT),
    )(ours, theirs, thin_ours, thin_theirs, coef, noise)


def receivers(observed, recv_tile, recv_cell, cell_count):
    tile_count = lax.axis_size(("gx", "gy"))
    highest = lax.Precision.HIGHEST
    tile_of = recv_tile[:, 0]
    per_tile = max(2, 2 * observed.shape[1] // tile_count)
    slot_count = tile_count * per_tile
    owner_hot = (tile_of[:, None] == jnp.arange(tile_count, dtype=jnp.int32)[None, :]).astype(
        jnp.int32
    )
    before = jnp.cumsum(owner_hot, 0) - owner_hot
    slot_of = tile_of * per_tile + jnp.sum(before * owner_hot, 1)
    routing = (slot_of[None, :] == jnp.arange(slot_count, dtype=jnp.int32)[:, None]).astype(
        jnp.float32
    )
    traces = jnp.pad(-observed[0][:, ::-1], ((0, 0), (DEPTH, 128 - DEPTH - STEPS)))
    marks = (recv_cell + 1).astype(jnp.float32)[:, None]
    lanes = jnp.arange(128, dtype=jnp.int32)[None, :]
    outgoing = jnp.dot(
        routing,
        jnp.where(lanes == MARK, marks, traces),
        precision=highest,
        preferred_element_type=jnp.float32,
    )
    arrived = lax.all_to_all(
        outgoing.reshape(tile_count, per_tile, 128),
        ("gx", "gy"),
        split_axis=0,
        concat_axis=0,
        tiled=True,
    ).reshape(slot_count, 128)
    cells = arrived[:, MARK].astype(jnp.int32) - 1
    picker = (jnp.arange(cell_count, dtype=jnp.int32)[:, None] == cells[None, :]).astype(
        jnp.float32
    )
    seen = jnp.dot(
        picker,
        jnp.where(lanes < THIN, arrived, 0.0),
        precision=highest,
        preferred_element_type=jnp.float32,
    )
    return jnp.sum(picker, 1, keepdims=True), seen


def local(
    coef, wave_now, wave_prev, adjoint_next, adjoint_after, noise, observed, recv_tile, recv_cell
):
    rows, cols, depth = coef.shape
    odd_x, odd_y = lax.axis_index("gx") % 2, lax.axis_index("gy") % 2
    parity = jnp.stack([odd_x, odd_y]).astype(jnp.int32)
    after = lambda value, *earlier: lax.optimization_barrier((value, earlier))[0]

    wave_fields = [wave_now[0], wave_prev[0], coef]
    adjoint_fields = [adjoint_next[0], adjoint_after[0]]
    sends = strips(parity, wave_fields, 0, K)
    wave_halos = swap("gx", *sends)
    counts, seen = receivers(after(observed, sends), recv_tile, recv_cell, rows * cols)
    speeds = jnp.pad(coef[:, :, :THIN], ((0, 0), (0, 0), (THIN, 128 - 2 * THIN)))
    sends = strips(parity, wave_fields, 1, K, wave_halos)
    wave_halos += swap("gy", *sends)
    sends = strips(after(parity, sends, counts, seen, speeds), adjoint_fields, 0, K)
    adjoint_halos = swap("gx", *sends)
    sends = strips(parity, adjoint_fields, 1, K, adjoint_halos)
    adjoint_halos += swap("gy", *sends)

    wave = (after(parity, sends), *wave_fields, wave_halos, wave_halos)
    now, then, *sends, laps_early, surface = run_block(*wave, False)
    wave_mid = swap("gx", *sends)
    adjoint = (after(parity, sends), *adjoint_fields, coef, adjoint_halos, wave_halos)
    later, latest, *late_sends, fields = run_block(*adjoint, True)
    sends = strips(after(parity, late_sends), [now, then], 1, K, wave_mid)
    wave_mid += swap("gy", *sends)
    adjoint_mid = swap("gx", *after(late_sends, sends))
    sends = strips(parity, [later, latest], 1, K, adjoint_mid)
    adjoint_mid += swap("gy", *sends)
    gradient = jnp.zeros(coef.shape, jnp.float32)
    wave = (after(parity, sends), now, then, coef, wave_mid, wave_halos)
    gradient, laps_late, surface = run_block(*wave, False, (fields, gradient, surface))
    thin = counts * surface.reshape(rows * cols, 128) + seen
    thin = thin.reshape(rows, cols, 128) + speeds
    sends = strips(parity, [thin], 0, STEPS)
    thin_halos = swap("gx", *sends)
    adjoint = (after(parity, sends), later, latest, coef, adjoint_mid, wave_halos)
    (gradient,) = run_block(*adjoint, True, (laps_early, gradient))
    shots = pairs(lax.axis_size("shot"), False)
    other = lax.ppermute(after(gradient, thin_halos), "shot", shots)
    sends = strips(after(parity, gradient), [thin], 1, STEPS, thin_halos)
    thin_halos += swap("gy", *sends)
    thin_gradient = run_thin(parity, thin, thin_halos, laps_early, laps_late)
    thin_other = lax.ppermute(thin_gradient, "shot", shots)
    return tuple(run_final(gradient, other, thin_gradient, thin_other, coef, noise))


def solution(mesh):
    return jax.shard_map(
        local,
        mesh=mesh,
        in_specs=(
            P("gx", "gy", None),
            P("shot", "gx", "gy", None),
            P("shot", "gx", "gy", None),
            P("shot", "gx", "gy", None),
            P("shot", "gx", "gy", None),
            P("gx", "gy", None),
            P("shot", ("gx", "gy"), None),
            P(("gx", "gy"), None),
            P(("gx", "gy")),
        ),
        out_specs=(P("gx", "gy", None), P("gx", "gy", None)),
        check_vma=False,
    )
```

```python
import functools
import math

import jax
import jax.numpy as jnp
from jax import lax
from jax.experimental import pallas as pl
from jax.experimental.pallas import tpu as pltpu
from jax.sharding import PartitionSpec as P

STEPS = 16
DEPTH = 2
K = 8
UNROLL = 8
THIN = 32
MARK = 64
COEF_HALOS = 6
THIN_UNROLL = 4
VMEM_LIMIT = 48 * 1024 * 1024
STRIP_VMEM_LIMIT = 16 * 1024 * 1024
FIRST_VMEM_LIMIT = 60 * 1024 * 1024

step_eta = 0.01
prior_prec = 4.0
prior_centre = 0.2


def pairs(count, odd):
    found = []
    for low in range(1 if odd else 0, count - 1, 2):
        found += [(low, low + 1), (low + 1, low)]
    return found


def swap(axis, first, second):
    count = lax.axis_size(axis)
    return (
        lax.ppermute(first, axis, pairs(count, False)),
        lax.ppermute(second, axis, pairs(count, True)),
    )


def strip_kernel(shape, axis, width, count, parity, *refs):
    fields, refs = refs[:count], refs[count:]
    received, sends, sems = refs[:-3], refs[-3:-1], refs[-1]
    rows, cols = shape[:2]
    far = (rows, cols)[axis] - width
    even = parity[axis] == 0
    copies = []

    def copy(source, target):
        copies.append(pltpu.make_async_copy(source, target, sems.at[len(copies)]))

    top = width + (rows if fields else 0)
    places = [jnp.where(parity[0] == 0, *pair) for pair in ((top, 0), (0, top))]
    for send, start in zip(sends, (jnp.where(even, far, 0), jnp.where(even, 0, far))):
        if axis == 0:
            for index, field in enumerate(fields):
                copy(field.at[pl.ds(start, width)], send.at[index])
            continue
        part = pl.ds(pl.multiple_of(start, 8), width)
        for index in range(send.shape[0]):
            if fields:
                inner = pl.ds(width if received else 0, rows)
                copy(fields[index].at[:, part], send.at[index, inner])
            for strip, place in zip(received, places):
                copy(strip.at[index, :, part], send.at[index, pl.ds(place, width)])
    run_copies(copies)


def strips(parity, fields, axis, width, received=(), limit=None):
    rows, cols, depth = fields[0].shape if fields else (0, received[0].shape[2], received[0].shape[3])
    count = len(fields) if fields else received[0].shape[0]
    height = rows + (2 * width if received else 0)
    shape = (count, width, cols, depth) if axis == 0 else (count, height, width, depth)
    send = jax.ShapeDtypeStruct(shape, jnp.float32)
    anywhere = pl.BlockSpec(memory_space=pl.ANY)
    copies = 2 * (len(fields) + count * len(received))
    return pl.pallas_call(
        functools.partial(strip_kernel, (rows, cols), axis, width, len(fields)),
        in_specs=[pl.BlockSpec(memory_space=pltpu.SMEM)]
        + [anywhere] * (len(fields) + len(received)),
        out_specs=[pl.BlockSpec(memory_space=pltpu.VMEM)] * 2,
        out_shape=[send, send],
        scratch_shapes=[pltpu.SemaphoreType.DMA((copies,))],
        compiler_params=pltpu.CompilerParams(vmem_limit_bytes=limit or STRIP_VMEM_LIMIT),
    )(parity, *fields, *received)


def halo_places(parity, shape, width, pad, halos):
    rows, cols = shape[:2]
    x_first = jnp.where(parity[0] == 0, rows + width, 0) + pad
    x_second = jnp.where(parity[0] == 0, 0, rows + width) + pad
    y_places = [
        pl.ds(pl.multiple_of(jnp.where(parity[1] == 0, *pair), 8), width)
        for pair in ((cols + width, 0), (0, cols + width))
    ]
    inner = pl.ds(width, cols)
    every, middle = pl.ds(pad, rows + 2 * width), pl.ds(pad + width, rows)
    ends = [(pl.ds(0, width), pl.ds(pad, width))]
    ends += [(pl.ds(width, width), pl.ds(pad + width + rows, width))]
    found = [(halos[0], (pl.ds(x_first, width), inner))]
    found += [(halos[1], (pl.ds(x_second, width), inner))]
    if len(halos) == 4:
        return found + [(halo, (every, place)) for halo, place in zip(halos[2:], y_places)]
    found += [(halo, (middle, place)) for halo, place in zip(halos[2:4], y_places)]
    for halo, place in zip(halos[4:], y_places):
        found += [(halo.at[part], (rows_at, place)) for part, rows_at in ends]
    return found


def run_copies(copies, between=None):
    for copy in copies:
        copy.start()
    if between is not None:
        between()
    for copy in copies:
        copy.wait()


def block_kernel(shape, adjoint, gather, halo_count, first_part, parity, *refs):
    rows, cols, depth = shape
    own_refs, refs = refs[:3], refs[3:]
    halo_refs, refs = refs[:halo_count], refs[halo_count:]
    if gather:
        factor, carried_in, refs = refs[0], refs[1], refs[2:]
    if gather:
        grad, refs = refs[0], refs[1:]
    else:
        newest, older, send_first, send_second, kept = refs[:5]
        refs = refs[5:]
    if gather and not adjoint:
        kept, refs = refs[0], refs[1:]
    if not adjoint:
        surface, refs = refs[0], refs[1:]
    first, second, coef, sems, out_sems = refs
    turn_of = pl.program_id(0)
    groups = cols // 8 + 2
    halves = depth // 128
    edge = K + 1
    lane = lax.broadcasted_iota(jnp.int32, (8, 128), 1)
    line = lax.broadcasted_iota(jnp.int32, (8, 128), 0)
    last_lane, first_lane = lane == 127, lane == 0
    last_line, first_line = line == 7, line == 0
    zero = jnp.zeros((8, 128), jnp.float32)

    @pl.when(turn_of == 0)
    def _():
        copies = []
        for index, (own, target) in enumerate(zip(own_refs, (first, second, coef))):
            halos = halo_refs[-COEF_HALOS:] if index == 2 else halo_refs[:-COEF_HALOS]
            part = 2 if index == 2 else first_part + index
            found = halo_places(parity, shape, K, 1, [halo.at[part] for halo in halos])
            found += [(own, (pl.ds(edge, rows), pl.ds(K, cols)))]
            for source, place in found:
                copies.append(
                    pltpu.make_async_copy(source, target.at[place], sems.at[len(copies)])
                )

        def pads():
            for field in (first, second, coef):
                field[0] = jnp.zeros(field.shape[1:], jnp.float32)
                field[rows + 2 * K + 1] = jnp.zeros(field.shape[1:], jnp.float32)
            if gather:
                grad[...] = carried_in[...] if adjoint else jnp.zeros_like(grad)
            if not adjoint:
                surface[...] = carried_in[...] if gather else jnp.zeros_like(surface)

        run_copies(copies, pads)
        if adjoint and not gather:

            def weigh(x, carried):
                first[x] = first[x] * coef[x]
                second[x] = second[x] * coef[x]
                return carried

            lax.fori_loop(1, rows + 2 * K + 1, weigh, 0)

    def load(source, x):
        return [
            [source[x, pl.ds(8 * g, 8), pl.ds(128 * h, 128)] for h in range(halves)]
            for g in range(groups)
        ]

    def row(x, target, half, inside, below, centre, above):
        ups = [[pltpu.roll(c, 7, 0) for c in line_of] for line_of in centre]
        downs = [[pltpu.roll(c, 1, 0) for c in line_of] for line_of in centre]
        done = []
        for g in range(groups):
            lefts = [pltpu.roll(c, 127, 1) for c in centre[g]]
            rights = [pltpu.roll(c, 1, 1) for c in centre[g]]
            for h in range(halves):
                c = centre[g][h]
                at = (x, pl.ds(8 * g, 8), pl.ds(128 * h, 128))
                up = jnp.where(last_line, ups[g + 1][h], ups[g][h]) if g + 1 < groups else ups[g][h]
                down = jnp.where(first_line, downs[g - 1][h], downs[g][h]) if g > 0 else downs[g][h]
                left = jnp.where(last_lane, lefts[h + 1] if h + 1 < halves else zero, lefts[h])
                right = jnp.where(first_lane, rights[h - 1] if h > 0 else zero, rights[h])
                lateral = (above[g][h] + below[g][h]) + (up + down)
                laplace = lateral + (left + right) - 6.0 * c
                fresh = (2.0 * c - target[at]) + coef[at] * laplace
                done.append((g, h, at, laplace, fresh))
        for g, h, at, laplace, fresh in done:
            target[at] = fresh
            if inside and 0 < g < groups - 1:
                mine = (x - edge, pl.ds(8 * g - 8, 8), pl.ds(128 * h, 128))
                term = fresh if adjoint else laplace
                if gather:
                    grad[mine] = grad[mine] + factor[(1 - half,) + mine] * term
                if not gather or (not adjoint and h == 0):
                    kept[(half,) + mine] = term
                if not adjoint and h == 0:
                    surface[mine] = jnp.where(lane == DEPTH, fresh, pltpu.roll(surface[mine], 1, 1))

    def sweep(source, target, half):
        def rows_from(begin, count, unroll, inside):
            def body(index, carried):
                below, centre = carried
                for offset in range(unroll):
                    x = begin + index * unroll + offset
                    above = load(source, x + 1)
                    row(x, target, half, inside, below, centre, above)
                    below, centre = centre, above
                return below, centre

            lax.fori_loop(0, count, body, (load(source, begin - 1), load(source, begin)))

        count = K // 2 - turn_of - half
        rows_from(edge - 2 * count, count, 2, False)
        rows_from(edge, rows // UNROLL, UNROLL, True)
        rows_from(edge + rows, count, 2, False)

    sweep(first, second, 0)
    sweep(second, first, 1)

    if not gather:

        @pl.when(turn_of == K // 2 - 1)
        def _():
            inner = pl.ds(K, cols)
            low, high = edge, edge + rows - K
            copies = []
            for index, (field, out) in enumerate(((first, newest), (second, older))):
                for source, target in (
                    (pl.ds(edge, rows), out),
                    (pl.ds(jnp.where(parity[0] == 0, high, low), K), send_first.at[index]),
                    (pl.ds(jnp.where(parity[0] == 0, low, high), K), send_second.at[index]),
                ):
                    copies.append(
                        pltpu.make_async_copy(
                            field.at[source, inner], target, out_sems.at[len(copies)]
                        )
                    )
            run_copies(copies)


def whole(shape):
    return pl.BlockSpec(shape, lambda step: (0,) * len(shape))


def run_block(parity, current, previous, coef, halos, coef_halos, adjoint, gather=None, first_part=0):
    rows, cols, depth = coef.shape
    extended = (rows + 2 * K + 2, cols + 2 * K, depth)
    any_spec = pl.BlockSpec(memory_space=pltpu.HBM)
    field = jax.ShapeDtypeStruct(coef.shape, jnp.float32)
    strips = jax.ShapeDtypeStruct((2, K, cols, depth), jnp.float32)
    flat = (rows, cols, 128)
    in_specs = [pl.BlockSpec(memory_space=pltpu.SMEM)] + [any_spec] * (3 + len(halos) + COEF_HALOS)
    operands = [parity, current, previous, coef, *halos, *coef_halos]
    if gather is not None:
        operands += gather
        in_specs += [
            pl.BlockSpec((2,) + coef.shape, lambda step: (K // 2 - 1 - step, 0, 0, 0)),
            whole(coef.shape if adjoint else flat),
        ]
        out_shape, out_specs = [field], [whole(coef.shape)]
    else:
        out_shape = [field, field, strips, strips]
        out_specs = [any_spec] * 4
    if gather is None or not adjoint:
        kept = flat if gather is not None else coef.shape
        out_shape += [jax.ShapeDtypeStruct((K,) + kept, jnp.float32)]
        out_specs += [pl.BlockSpec((2,) + kept, lambda step: (step, 0, 0, 0))]
    if not adjoint:
        out_shape += [jax.ShapeDtypeStruct(flat, jnp.float32)]
        out_specs += [whole(flat)]
    return pl.pallas_call(
        functools.partial(
            block_kernel,
            coef.shape,
            adjoint,
            gather is not None,
            len(halos) + COEF_HALOS,
            first_part,
        ),
        grid=(K // 2,),
        in_specs=in_specs,
        out_specs=out_specs,
        out_shape=out_shape,
        scratch_shapes=[pltpu.VMEM(extended, jnp.float32)] * 3
        + [pltpu.SemaphoreType.DMA((27,)), pltpu.SemaphoreType.DMA((6,))],
        cost_estimate=pl.CostEstimate(flops=10**8, bytes_accessed=6 * 10**7, transcendentals=0),
        compiler_params=pltpu.CompilerParams(vmem_limit_bytes=VMEM_LIMIT),
    )(*operands)


def thin_kernel(shape, parity, own, *refs):
    halo_refs, refs = refs[:4], refs[4:]
    laps_early, laps_late, packed_out, tile, first, second, coef, inject, grad, sems = refs
    rows, cols = shape[:2]
    turn_of = pl.program_id(0)
    blocks = 128 // THIN
    span = (rows + 2 * STEPS) // blocks
    groups = (cols + 2 * STEPS) // 8
    margin = STEPS // 8
    lane = lax.broadcasted_iota(jnp.int32, (8, 128), 1)
    line = lax.broadcasted_iota(jnp.int32, (8, 128), 0)
    in_block = lane % THIN
    last_lane, first_lane = in_block == THIN - 1, in_block == 0
    last_line, first_line = line == 7, line == 0

    def rows8(g):
        return pl.ds(8 * g, 8)

    @pl.when(turn_of == 0)
    def _():
        found = halo_places(parity, shape, STEPS, 0, [halo.at[0] for halo in halo_refs])
        found += [(own, (pl.ds(STEPS, rows), pl.ds(STEPS, cols)))]
        run_copies(
            [
                pltpu.make_async_copy(source, tile.at[place], sems.at[index])
                for index, (source, place) in enumerate(found)
            ]
        )
        first[...] = jnp.zeros_like(first)
        second[...] = jnp.zeros_like(second)
        grad[...] = jnp.zeros_like(grad)

        def pack(i, carried):
            for g in range(groups):
                forces, speeds = jnp.zeros((8, 128), jnp.float32), jnp.zeros((8, 128), jnp.float32)
                for block in range(blocks):
                    value = tile[block * span + i, rows8(g), :]
                    here = lane // THIN == block
                    forces = jnp.where(here, pltpu.roll(value, THIN * block, 1), forces)
                    speeds = jnp.where(
                        here, pltpu.roll(value, (THIN * block - THIN) % 128, 1), speeds
                    )
                inject[i, rows8(g), :] = forces
                coef[i, rows8(g), :] = speeds
            return carried

        lax.fori_loop(0, span, pack, 0)

    def sweep(source, target, half, laps):
        def load(i):
            return [source[i, rows8(g), :] for g in range(groups)]

        def body(index, carried):
            below, centre = carried
            for offset in range(THIN_UNROLL):
                i = index * THIN_UNROLL + offset
                above = load(i + 2)
                ups = [pltpu.roll(c, 7, 0) for c in centre]
                downs = [pltpu.roll(c, 1, 0) for c in centre]
                done = []
                for g, c in enumerate(centre):
                    up = jnp.where(last_line, ups[g + 1], ups[g]) if g + 1 < groups else ups[g]
                    down = jnp.where(first_line, downs[g - 1], downs[g]) if g > 0 else downs[g]
                    left = jnp.where(last_lane, 0.0, pltpu.roll(c, 127, 1))
                    right = jnp.where(first_lane, 0.0, pltpu.roll(c, 1, 1))
                    laplace = (above[g] + below[g]) + (up + down) + (left + right) - 6.0 * c
                    force = inject[i, rows8(g), :]
                    forced = laplace + jnp.where(in_block == DEPTH, force, 0.0)
                    fresh = (2.0 * c - target[i + 1, rows8(g), :]) + coef[i, rows8(g), :] * forced
                    done.append((g, pltpu.roll(force, 127, 1), fresh))
                for g, force, fresh in done:
                    inject[i, rows8(g), :] = force
                    target[i + 1, rows8(g), :] = fresh
                for g, _, fresh in done[margin : groups - margin]:
                    for block in range(rows // span):
                        moved = pltpu.roll(fresh, 128 - THIN * (block + STEPS // span), 1)
                        at = (block * span + i, rows8(g - margin), slice(None))
                        grad[at] = grad[at] + laps[(1 - half,) + at] * moved
                below, centre = centre, above
            return below, centre

        lax.fori_loop(0, span // THIN_UNROLL, body, (load(0), load(1)))
        for g in range(groups):
            target[0, rows8(g), :] = pltpu.roll(target[span, rows8(g), :], THIN, 1)
            target[span + 1, rows8(g), :] = pltpu.roll(target[1, rows8(g), :], 128 - THIN, 1)

    @pl.when(turn_of < STEPS // 4)
    def _():
        sweep(first, second, 0, laps_late)
        sweep(second, first, 1, laps_late)

    @pl.when(turn_of >= STEPS // 4)
    def _():
        sweep(first, second, 0, laps_early)
        sweep(second, first, 1, laps_early)

    @pl.when(turn_of == STEPS // 2 - 1)
    def _():
        height = rows // blocks
        for p in range(height):
            for g in range(cols // 8):
                value = jnp.zeros((8, 128), jnp.float32)
                for block in range(blocks):
                    moved = pltpu.roll(grad[block * height + p, rows8(g), :], THIN * block, 1)
                    value = jnp.where(lane // THIN == block, moved, value)
                packed_out[p, rows8(g), :] = value


def run_thin(parity, own, halos, laps_early, laps_late):
    rows, cols = own.shape[:2]
    extended = (rows + 2 * STEPS, cols + 2 * STEPS, 128)
    span = extended[0] * THIN // 128
    packed = (rows * THIN // 128, cols, 128)
    half = STEPS // 4
    any_spec = pl.BlockSpec(memory_space=pltpu.HBM)
    return pl.pallas_call(
        functools.partial(thin_kernel, own.shape),
        grid=(STEPS // 2,),
        in_specs=[pl.BlockSpec(memory_space=pltpu.SMEM)]
        + [any_spec] * 5
        + [
            pl.BlockSpec(
                (2, rows, cols, 128), lambda step: (jnp.minimum(half - 1, 2 * half - 1 - step), 0, 0, 0)
            ),
            pl.BlockSpec(
                (2, rows, cols, 128), lambda step: (jnp.maximum(0, half - 1 - step), 0, 0, 0)
            ),
        ],
        out_specs=whole(packed),
        out_shape=jax.ShapeDtypeStruct(packed, jnp.float32),
        scratch_shapes=[
            pltpu.VMEM(extended, jnp.float32),
            pltpu.VMEM((span + 2, extended[1], 128), jnp.float32),
            pltpu.VMEM((span + 2, extended[1], 128), jnp.float32),
            pltpu.VMEM((span, extended[1], 128), jnp.float32),
            pltpu.VMEM((span, extended[1], 128), jnp.float32),
            pltpu.VMEM((rows, cols, 128), jnp.float32),
            pltpu.SemaphoreType.DMA((5,)),
        ],
        cost_estimate=pl.CostEstimate(flops=10**8, bytes_accessed=5 * 10**7, transcendentals=0),
        compiler_params=pltpu.CompilerParams(vmem_limit_bytes=VMEM_LIMIT),
    )(parity, own, *halos, laps_early, laps_late)


def final_kernel(ours, theirs, thin_ours, thin_theirs, coef, noise, sample, total):
    block = pl.program_id(0)
    lane = lax.broadcasted_iota(jnp.int32, (8, 128), 1)
    for p in range(coef.shape[0]):
        for g in range(coef.shape[1] // 8):
            lines = pl.ds(8 * g, 8)
            thin = thin_ours[p, lines, :] + thin_theirs[p, lines, :]
            thin = jnp.where(lane < THIN, pltpu.roll(thin, lax.rem(128 - THIN * block, 128), 1), 0.0)
            for h in range(coef.shape[2] // 128):
                at = (p, lines, pl.ds(128 * h, 128))
                summed = ours[at] + theirs[at]
                if h == 0:
                    summed = summed + thin
                speed = coef[at]
                gradient = summed / speed
                total[at] = gradient
                sample[at] = (
                    speed
                    + step_eta * (prior_prec * (prior_centre - speed) - gradient)
                    + math.sqrt(2.0 * step_eta) * noise[at]
                )


def run_final(ours, theirs, thin_ours, thin_theirs, coef, noise):
    blocks = 128 // THIN
    part = pl.BlockSpec((coef.shape[0] // blocks,) + coef.shape[1:], lambda step: (step, 0, 0))
    thin = whole(thin_ours.shape)
    field = jax.ShapeDtypeStruct(coef.shape, jnp.float32)
    return pl.pallas_call(
        final_kernel,
        grid=(blocks,),
        in_specs=[part, part, thin, thin, part, part],
        out_specs=[part, part],
        out_shape=[field, field],
        compiler_params=pltpu.CompilerParams(vmem_limit_bytes=VMEM_LIMIT),
    )(ours, theirs, thin_ours, thin_theirs, coef, noise)


def receivers(observed, recv_tile, recv_cell, cell_count):
    tile_count = lax.axis_size(("gx", "gy"))
    highest = lax.Precision.HIGHEST
    tile_of = recv_tile[:, 0]
    per_tile = max(2, 2 * observed.shape[1] // tile_count)
    slot_count = tile_count * per_tile
    owner_hot = (tile_of[:, None] == jnp.arange(tile_count, dtype=jnp.int32)[None, :]).astype(
        jnp.int32
    )
    before = jnp.cumsum(owner_hot, 0) - owner_hot
    slot_of = tile_of * per_tile + jnp.sum(before * owner_hot, 1)
    routing = (slot_of[None, :] == jnp.arange(slot_count, dtype=jnp.int32)[:, None]).astype(
        jnp.float32
    )
    traces = jnp.pad(-observed[0][:, ::-1], ((0, 0), (DEPTH, 128 - DEPTH - STEPS)))
    marks = (recv_cell + 1).astype(jnp.float32)[:, None]
    lanes = jnp.arange(128, dtype=jnp.int32)[None, :]
    outgoing = jnp.dot(
        routing,
        jnp.where(lanes == MARK, marks, traces),
        precision=highest,
        preferred_element_type=jnp.float32,
    )
    arrived = lax.all_to_all(
        outgoing.reshape(tile_count, per_tile, 128),
        ("gx", "gy"),
        split_axis=0,
        concat_axis=0,
        tiled=True,
    ).reshape(slot_count, 128)
    cells = arrived[:, MARK].astype(jnp.int32) - 1
    picker = (jnp.arange(cell_count, dtype=jnp.int32)[:, None] == cells[None, :]).astype(
        jnp.float32
    )
    seen = jnp.dot(
        picker,
        jnp.where(lanes < THIN, arrived, 0.0),
        precision=highest,
        preferred_element_type=jnp.float32,
    )
    return jnp.sum(picker, 1, keepdims=True), seen


def local(
    coef, wave_now, wave_prev, adjoint_next, adjoint_after, noise, observed, recv_tile, recv_cell
):
    rows, cols, depth = coef.shape
    odd_x, odd_y = lax.axis_index("gx") % 2, lax.axis_index("gy") % 2
    parity = jnp.stack([odd_x, odd_y]).astype(jnp.int32)
    after = lambda value, *earlier: lax.optimization_barrier((value, earlier))[0]

    fields = [wave_now[0], wave_prev[0], coef, adjoint_next[0], adjoint_after[0]]
    sends = strips(parity, fields, 0, K, limit=FIRST_VMEM_LIMIT)
    halos = swap("gx", *sends)
    early = after(parity, sends)
    sends_y = strips(early, fields, 1, K)
    halos += swap("gy", *sends_y)
    counts, seen = receivers(after(observed, sends_y), recv_tile, recv_cell, rows * cols)
    speeds = jnp.pad(coef[:, :, :THIN], ((0, 0), (0, 0), (THIN, 128 - 2 * THIN)))
    sends = strips(after(parity, counts, seen, speeds), [], 1, K, halos[:2])
    halos += swap("gy", *sends)

    wave = (after(parity, sends), *fields[:3], halos, halos)
    now, then, *sends, laps_early, surface = run_block(*wave, False)
    wave_mid = swap("gx", *sends)
    sends_y = strips(after(parity, sends), [now, then], 1, K)
    wave_mid += swap("gy", *sends_y)
    adjoint = (after(parity, sends_y), *fields[3:], coef, halos, halos)
    later, latest, *late_sends, ahead = run_block(*adjoint, True, first_part=3)
    sends = strips(after(parity, late_sends), [], 1, K, wave_mid[:2])
    wave_mid += swap("gy", *sends)
    adjoint_mid = swap("gx", *after(late_sends, sends))
    wave = (parity, now, then, coef, wave_mid, halos)
    gradient, laps_late, surface = run_block(*wave, False, (ahead, surface))
    thin = counts * surface.reshape(rows * cols, 128) + seen
    thin = thin.reshape(rows, cols, 128) + speeds
    sends = strips(after(parity, surface), [later, latest], 1, K, adjoint_mid)
    adjoint_mid += swap("gy", *sends)
    sends = strips(parity, [thin], 0, STEPS)
    thin_halos = swap("gx", *sends)
    sends = strips(parity, [thin], 1, STEPS, thin_halos)
    thin_halos += swap("gy", *sends)
    adjoint = (after(parity, sends), later, latest, coef, adjoint_mid, halos)
    (gradient,) = run_block(*adjoint, True, (laps_early, gradient))
    shots = pairs(lax.axis_size("shot"), False)
    other = lax.ppermute(after(gradient, thin_halos), "shot", shots)
    thin_gradient = run_thin(parity, thin, thin_halos, laps_early, laps_late)
    thin_other = lax.ppermute(thin_gradient, "shot", shots)
    return tuple(run_final(gradient, other, thin_gradient, thin_other, coef, noise))


def solution(mesh):
    return jax.shard_map(
        local,
        mesh=mesh,
        in_specs=(
            P("gx", "gy", None),
            P("shot", "gx", "gy", None),
            P("shot", "gx", "gy", None),
            P("shot", "gx", "gy", None),
            P("shot", "gx", "gy", None),
            P("gx", "gy", None),
            P("shot", ("gx", "gy"), None),
            P(("gx", "gy"), None),
            P(("gx", "gy")),
        ),
        out_specs=(P("gx", "gy", None), P("gx", "gy", None)),
        check_vma=False,
    )
```

```python
import functools
import math

import jax
import jax.numpy as jnp
from jax import lax
from jax.experimental import pallas as pl
from jax.experimental.pallas import tpu as pltpu
from jax.sharding import PartitionSpec as P

STEPS = 16
DEPTH = 2
K = 8
UNROLL = 32
THIN = 32
MARK = 64
COEF_HALOS = 6
THIN_UNROLL = 4
VMEM_LIMIT = 48 * 1024 * 1024
STRIP_VMEM_LIMIT = 16 * 1024 * 1024
FIRST_VMEM_LIMIT = 60 * 1024 * 1024

step_eta = 0.01
prior_prec = 4.0
prior_centre = 0.2


def pairs(count, odd):
    found = []
    for low in range(1 if odd else 0, count - 1, 2):
        found += [(low, low + 1), (low + 1, low)]
    return found


def swap(axis, first, second):
    count = lax.axis_size(axis)
    return (
        lax.ppermute(first, axis, pairs(count, False)),
        lax.ppermute(second, axis, pairs(count, True)),
    )


def strip_kernel(shape, axis, width, count, parity, *refs):
    fields, refs = refs[:count], refs[count:]
    received, sends, sems = refs[:-3], refs[-3:-1], refs[-1]
    rows, cols = shape[:2]
    far = (rows, cols)[axis] - width
    even = parity[axis] == 0
    copies = []

    def copy(source, target):
        copies.append(pltpu.make_async_copy(source, target, sems.at[len(copies)]))

    top = width + (rows if fields else 0)
    places = [jnp.where(parity[0] == 0, *pair) for pair in ((top, 0), (0, top))]
    for send, start in zip(sends, (jnp.where(even, far, 0), jnp.where(even, 0, far))):
        if axis == 0:
            for index, field in enumerate(fields):
                copy(field.at[pl.ds(start, width)], send.at[index])
            continue
        part = pl.ds(pl.multiple_of(start, 8), width)
        for index in range(send.shape[0]):
            if fields:
                inner = pl.ds(width if received else 0, rows)
                copy(fields[index].at[:, part], send.at[index, inner])
            for strip, place in zip(received, places):
                copy(strip.at[index, :, part], send.at[index, pl.ds(place, width)])
    run_copies(copies)


def strips(parity, fields, axis, width, received=(), limit=None):
    rows, cols, depth = fields[0].shape if fields else (0, received[0].shape[2], received[0].shape[3])
    count = len(fields) if fields else received[0].shape[0]
    height = rows + (2 * width if received else 0)
    shape = (count, width, cols, depth) if axis == 0 else (count, height, width, depth)
    send = jax.ShapeDtypeStruct(shape, jnp.float32)
    anywhere = pl.BlockSpec(memory_space=pl.ANY)
    copies = 2 * (len(fields) + count * len(received))
    return pl.pallas_call(
        functools.partial(strip_kernel, (rows, cols), axis, width, len(fields)),
        in_specs=[pl.BlockSpec(memory_space=pltpu.SMEM)]
        + [anywhere] * (len(fields) + len(received)),
        out_specs=[pl.BlockSpec(memory_space=pltpu.VMEM)] * 2,
        out_shape=[send, send],
        scratch_shapes=[pltpu.SemaphoreType.DMA((copies,))],
        compiler_params=pltpu.CompilerParams(vmem_limit_bytes=limit or STRIP_VMEM_LIMIT),
    )(parity, *fields, *received)


def halo_places(parity, shape, width, pad, halos):
    rows, cols = shape[:2]
    x_first = jnp.where(parity[0] == 0, rows + width, 0) + pad
    x_second = jnp.where(parity[0] == 0, 0, rows + width) + pad
    y_places = [
        pl.ds(pl.multiple_of(jnp.where(parity[1] == 0, *pair), 8), width)
        for pair in ((cols + width, 0), (0, cols + width))
    ]
    inner = pl.ds(width, cols)
    every, middle = pl.ds(pad, rows + 2 * width), pl.ds(pad + width, rows)
    ends = [(pl.ds(0, width), pl.ds(pad, width))]
    ends += [(pl.ds(width, width), pl.ds(pad + width + rows, width))]
    found = [(halos[0], (pl.ds(x_first, width), inner))]
    found += [(halos[1], (pl.ds(x_second, width), inner))]
    if len(halos) == 4:
        return found + [(halo, (every, place)) for halo, place in zip(halos[2:], y_places)]
    found += [(halo, (middle, place)) for halo, place in zip(halos[2:4], y_places)]
    for halo, place in zip(halos[4:], y_places):
        found += [(halo.at[part], (rows_at, place)) for part, rows_at in ends]
    return found


def run_copies(copies, between=None):
    for copy in copies:
        copy.start()
    if between is not None:
        between()
    for copy in copies:
        copy.wait()


def block_kernel(shape, adjoint, gather, halo_count, first_part, parity, *refs):
    rows, cols, depth = shape
    own_refs, refs = refs[:3], refs[3:]
    halo_refs, refs = refs[:halo_count], refs[halo_count:]
    if gather:
        factor, carried_in, refs = refs[0], refs[1], refs[2:]
    if gather:
        grad, refs = refs[0], refs[1:]
    else:
        newest, older, send_first, send_second, kept = refs[:5]
        refs = refs[5:]
    if gather and not adjoint:
        kept, refs = refs[0], refs[1:]
    if not adjoint:
        surface, refs = refs[0], refs[1:]
    first, second, coef, sems, out_sems = refs
    turn_of = pl.program_id(0)
    groups = cols // 8 + 2
    halves = depth // 128
    edge = K + 1
    lane = lax.broadcasted_iota(jnp.int32, (8, 128), 1)
    line = lax.broadcasted_iota(jnp.int32, (8, 128), 0)
    last_lane, first_lane = lane == 127, lane == 0
    last_line, first_line = line == 7, line == 0
    zero = jnp.zeros((8, 128), jnp.float32)

    @pl.when(turn_of == 0)
    def _():
        copies = []
        for index, (own, target) in enumerate(zip(own_refs, (first, second, coef))):
            halos = halo_refs[-COEF_HALOS:] if index == 2 else halo_refs[:-COEF_HALOS]
            part = 2 if index == 2 else first_part + index
            found = halo_places(parity, shape, K, 1, [halo.at[part] for halo in halos])
            found += [(own, (pl.ds(edge, rows), pl.ds(K, cols)))]
            for source, place in found:
                copies.append(
                    pltpu.make_async_copy(source, target.at[place], sems.at[len(copies)])
                )

        def pads():
            for field in (first, second, coef):
                field[0] = jnp.zeros(field.shape[1:], jnp.float32)
                field[rows + 2 * K + 1] = jnp.zeros(field.shape[1:], jnp.float32)
            if gather:
                grad[...] = carried_in[...] if adjoint else jnp.zeros_like(grad)
            if not adjoint:
                surface[...] = carried_in[...] if gather else jnp.zeros_like(surface)

        run_copies(copies, pads)
        if adjoint and not gather:

            def weigh(x, carried):
                first[x] = first[x] * coef[x]
                second[x] = second[x] * coef[x]
                return carried

            lax.fori_loop(1, rows + 2 * K + 1, weigh, 0)

    def load(source, x):
        return [
            [source[x, pl.ds(8 * g, 8), pl.ds(128 * h, 128)] for h in range(halves)]
            for g in range(groups)
        ]

    def row(x, target, half, inside, below, centre, above, short):
        ups = [[pltpu.roll(c, 7, 0) for c in line_of] for line_of in centre]
        downs = [[pltpu.roll(c, 1, 0) for c in line_of] for line_of in centre]
        done = []
        for g in range(1, groups - 1) if short else range(groups):
            lefts = [pltpu.roll(c, 127, 1) for c in centre[g]]
            rights = [pltpu.roll(c, 1, 1) for c in centre[g]]
            for h in range(halves):
                c = centre[g][h]
                at = (x, pl.ds(8 * g, 8), pl.ds(128 * h, 128))
                up = jnp.where(last_line, ups[g + 1][h], ups[g][h]) if g + 1 < groups else ups[g][h]
                down = jnp.where(first_line, downs[g - 1][h], downs[g][h]) if g > 0 else downs[g][h]
                left = jnp.where(last_lane, lefts[h + 1] if h + 1 < halves else zero, lefts[h])
                right = jnp.where(first_lane, rights[h - 1] if h > 0 else zero, rights[h])
                lateral = (above[g][h] + below[g][h]) + (up + down)
                laplace = lateral + (left + right) - 6.0 * c
                fresh = (2.0 * c - target[at]) + coef[at] * laplace
                done.append((g, h, at, laplace, fresh))
        for g, h, at, laplace, fresh in done:
            target[at] = fresh
            if inside and 0 < g < groups - 1:
                mine = (x - edge, pl.ds(8 * g - 8, 8), pl.ds(128 * h, 128))
                term = fresh if adjoint else laplace
                if gather:
                    grad[mine] = grad[mine] + factor[(1 - half,) + mine] * term
                if not gather or (not adjoint and h == 0):
                    kept[(half,) + mine] = term
                if not adjoint and h == 0:
                    surface[mine] = jnp.where(lane == DEPTH, fresh, pltpu.roll(surface[mine], 1, 1))

    def some_rows(source, target, half, first_row, many, inside, carried, short=False):
        below, centre = carried
        for x in range(many):
            above = load(source, first_row + x + 1)
            row(first_row + x, target, half, inside, below, centre, above, short)
            below, centre = centre, above
        return below, centre

    def start_at(source, x):
        return load(source, x - 1), load(source, x)

    def halo_rows(source, target, half, count):
        def body(index, carried):
            for x in (edge - 2 * count + 2 * index, edge + rows + 2 * index):
                some_rows(source, target, half, x, 2, False, start_at(source, x))
            return carried

        lax.fori_loop(0, count, body, 0)

    def own_rows(source, target, half, short=False):
        def body(index, carried):
            x = edge + index * UNROLL
            return some_rows(source, target, half, x, UNROLL, True, carried, short)

        lax.fori_loop(0, rows // UNROLL, body, start_at(source, edge))

    last = turn_of == K // 2 - 1
    halo_rows(first, second, 0, K // 2 - turn_of)
    own_rows(first, second, 0)

    @pl.when(jnp.logical_not(last))
    def _():
        halo_rows(second, first, 1, K // 2 - 1 - turn_of)
        own_rows(second, first, 1)

    @pl.when(last)
    def _():
        own_rows(second, first, 1, True)

    if not gather:

        @pl.when(turn_of == K // 2 - 1)
        def _():
            inner = pl.ds(K, cols)
            low, high = edge, edge + rows - K
            copies = []
            for index, (field, out) in enumerate(((first, newest), (second, older))):
                for source, target in (
                    (pl.ds(edge, rows), out),
                    (pl.ds(jnp.where(parity[0] == 0, high, low), K), send_first.at[index]),
                    (pl.ds(jnp.where(parity[0] == 0, low, high), K), send_second.at[index]),
                ):
                    copies.append(
                        pltpu.make_async_copy(
                            field.at[source, inner], target, out_sems.at[len(copies)]
                        )
                    )
            run_copies(copies)


def whole(shape):
    return pl.BlockSpec(shape, lambda step: (0,) * len(shape))


def run_block(parity, current, previous, coef, halos, coef_halos, adjoint, gather=None, first_part=0):
    rows, cols, depth = coef.shape
    extended = (rows + 2 * K + 2, cols + 2 * K, depth)
    any_spec = pl.BlockSpec(memory_space=pltpu.HBM)
    field = jax.ShapeDtypeStruct(coef.shape, jnp.float32)
    strips = jax.ShapeDtypeStruct((2, K, cols, depth), jnp.float32)
    flat = (rows, cols, 128)
    in_specs = [pl.BlockSpec(memory_space=pltpu.SMEM)] + [any_spec] * (3 + len(halos) + COEF_HALOS)
    operands = [parity, current, previous, coef, *halos, *coef_halos]
    if gather is not None:
        operands += gather
        in_specs += [
            pl.BlockSpec((2,) + coef.shape, lambda step: (K // 2 - 1 - step, 0, 0, 0)),
            whole(coef.shape if adjoint else flat),
        ]
        out_shape, out_specs = [field], [whole(coef.shape)]
    else:
        out_shape = [field, field, strips, strips]
        out_specs = [any_spec] * 4
    if gather is None or not adjoint:
        kept = flat if gather is not None else coef.shape
        out_shape += [jax.ShapeDtypeStruct((K,) + kept, jnp.float32)]
        out_specs += [pl.BlockSpec((2,) + kept, lambda step: (step, 0, 0, 0))]
    if not adjoint:
        out_shape += [jax.ShapeDtypeStruct(flat, jnp.float32)]
        out_specs += [whole(flat)]
    return pl.pallas_call(
        functools.partial(
            block_kernel,
            coef.shape,
            adjoint,
            gather is not None,
            len(halos) + COEF_HALOS,
            first_part,
        ),
        grid=(K // 2,),
        in_specs=in_specs,
        out_specs=out_specs,
        out_shape=out_shape,
        scratch_shapes=[pltpu.VMEM(extended, jnp.float32)] * 3
        + [pltpu.SemaphoreType.DMA((27,)), pltpu.SemaphoreType.DMA((6,))],
        cost_estimate=pl.CostEstimate(flops=10**8, bytes_accessed=6 * 10**7, transcendentals=0),
        compiler_params=pltpu.CompilerParams(vmem_limit_bytes=VMEM_LIMIT),
    )(*operands)


def thin_kernel(shape, parity, own, *refs):
    halo_refs, refs = refs[:4], refs[4:]
    laps_early, laps_late, packed_out, tile, first, second, coef, inject, grad, sems = refs
    rows, cols = shape[:2]
    turn_of = pl.program_id(0)
    blocks = 128 // THIN
    span = (rows + 2 * STEPS) // blocks
    groups = (cols + 2 * STEPS) // 8
    margin = STEPS // 8
    lane = lax.broadcasted_iota(jnp.int32, (8, 128), 1)
    line = lax.broadcasted_iota(jnp.int32, (8, 128), 0)
    in_block = lane % THIN
    last_lane, first_lane = in_block == THIN - 1, in_block == 0
    last_line, first_line = line == 7, line == 0

    def rows8(g):
        return pl.ds(8 * g, 8)

    @pl.when(turn_of == 0)
    def _():
        found = halo_places(parity, shape, STEPS, 0, [halo.at[0] for halo in halo_refs])
        found += [(own, (pl.ds(STEPS, rows), pl.ds(STEPS, cols)))]
        run_copies(
            [
                pltpu.make_async_copy(source, tile.at[place], sems.at[index])
                for index, (source, place) in enumerate(found)
            ]
        )
        first[...] = jnp.zeros_like(first)
        second[...] = jnp.zeros_like(second)
        grad[...] = jnp.zeros_like(grad)

        def pack(i, carried):
            for g in range(groups):
                forces, speeds = jnp.zeros((8, 128), jnp.float32), jnp.zeros((8, 128), jnp.float32)
                for block in range(blocks):
                    value = tile[block * span + i, rows8(g), :]
                    here = lane // THIN == block
                    forces = jnp.where(here, pltpu.roll(value, THIN * block, 1), forces)
                    speeds = jnp.where(
                        here, pltpu.roll(value, (THIN * block - THIN) % 128, 1), speeds
                    )
                inject[i, rows8(g), :] = forces
                coef[i, rows8(g), :] = speeds
            return carried

        lax.fori_loop(0, span, pack, 0)

    def sweep(source, target, half, laps):
        def load(i):
            return [source[i, rows8(g), :] for g in range(groups)]

        def body(index, carried):
            below, centre = carried
            for offset in range(THIN_UNROLL):
                i = index * THIN_UNROLL + offset
                above = load(i + 2)
                ups = [pltpu.roll(c, 7, 0) for c in centre]
                downs = [pltpu.roll(c, 1, 0) for c in centre]
                done = []
                for g, c in enumerate(centre):
                    up = jnp.where(last_line, ups[g + 1], ups[g]) if g + 1 < groups else ups[g]
                    down = jnp.where(first_line, downs[g - 1], downs[g]) if g > 0 else downs[g]
                    left = jnp.where(last_lane, 0.0, pltpu.roll(c, 127, 1))
                    right = jnp.where(first_lane, 0.0, pltpu.roll(c, 1, 1))
                    laplace = (above[g] + below[g]) + (up + down) + (left + right) - 6.0 * c
                    force = inject[i, rows8(g), :]
                    forced = laplace + jnp.where(in_block == DEPTH, force, 0.0)
                    fresh = (2.0 * c - target[i + 1, rows8(g), :]) + coef[i, rows8(g), :] * forced
                    done.append((g, pltpu.roll(force, 127, 1), fresh))
                for g, force, fresh in done:
                    inject[i, rows8(g), :] = force
                    target[i + 1, rows8(g), :] = fresh
                for g, _, fresh in done[margin : groups - margin]:
                    for block in range(rows // span):
                        moved = pltpu.roll(fresh, 128 - THIN * (block + STEPS // span), 1)
                        at = (block * span + i, rows8(g - margin), slice(None))
                        grad[at] = grad[at] + laps[(1 - half,) + at] * moved
                below, centre = centre, above
            return below, centre

        lax.fori_loop(0, span // THIN_UNROLL, body, (load(0), load(1)))
        for g in range(groups):
            target[0, rows8(g), :] = pltpu.roll(target[span, rows8(g), :], THIN, 1)
            target[span + 1, rows8(g), :] = pltpu.roll(target[1, rows8(g), :], 128 - THIN, 1)

    @pl.when(turn_of < STEPS // 4)
    def _():
        sweep(first, second, 0, laps_late)
        sweep(second, first, 1, laps_late)

    @pl.when(turn_of >= STEPS // 4)
    def _():
        sweep(first, second, 0, laps_early)
        sweep(second, first, 1, laps_early)

    @pl.when(turn_of == STEPS // 2 - 1)
    def _():
        height = rows // blocks
        for p in range(height):
            for g in range(cols // 8):
                value = jnp.zeros((8, 128), jnp.float32)
                for block in range(blocks):
                    moved = pltpu.roll(grad[block * height + p, rows8(g), :], THIN * block, 1)
                    value = jnp.where(lane // THIN == block, moved, value)
                packed_out[p, rows8(g), :] = value


def run_thin(parity, own, halos, laps_early, laps_late):
    rows, cols = own.shape[:2]
    extended = (rows + 2 * STEPS, cols + 2 * STEPS, 128)
    span = extended[0] * THIN // 128
    packed = (rows * THIN // 128, cols, 128)
    half = STEPS // 4
    any_spec = pl.BlockSpec(memory_space=pltpu.HBM)
    return pl.pallas_call(
        functools.partial(thin_kernel, own.shape),
        grid=(STEPS // 2,),
        in_specs=[pl.BlockSpec(memory_space=pltpu.SMEM)]
        + [any_spec] * 5
        + [
            pl.BlockSpec(
                (2, rows, cols, 128), lambda step: (jnp.minimum(half - 1, 2 * half - 1 - step), 0, 0, 0)
            ),
            pl.BlockSpec(
                (2, rows, cols, 128), lambda step: (jnp.maximum(0, half - 1 - step), 0, 0, 0)
            ),
        ],
        out_specs=whole(packed),
        out_shape=jax.ShapeDtypeStruct(packed, jnp.float32),
        scratch_shapes=[
            pltpu.VMEM(extended, jnp.float32),
            pltpu.VMEM((span + 2, extended[1], 128), jnp.float32),
            pltpu.VMEM((span + 2, extended[1], 128), jnp.float32),
            pltpu.VMEM((span, extended[1], 128), jnp.float32),
            pltpu.VMEM((span, extended[1], 128), jnp.float32),
            pltpu.VMEM((rows, cols, 128), jnp.float32),
            pltpu.SemaphoreType.DMA((5,)),
        ],
        cost_estimate=pl.CostEstimate(flops=10**8, bytes_accessed=5 * 10**7, transcendentals=0),
        compiler_params=pltpu.CompilerParams(vmem_limit_bytes=VMEM_LIMIT),
    )(parity, own, *halos, laps_early, laps_late)


def final_kernel(ours, theirs, thin_ours, thin_theirs, coef, noise, sample, total):
    block = pl.program_id(0)
    lane = lax.broadcasted_iota(jnp.int32, (8, 128), 1)
    for p in range(coef.shape[0]):
        for g in range(coef.shape[1] // 8):
            lines = pl.ds(8 * g, 8)
            thin = thin_ours[p, lines, :] + thin_theirs[p, lines, :]
            thin = jnp.where(lane < THIN, pltpu.roll(thin, lax.rem(128 - THIN * block, 128), 1), 0.0)
            for h in range(coef.shape[2] // 128):
                at = (p, lines, pl.ds(128 * h, 128))
                summed = ours[at] + theirs[at]
                if h == 0:
                    summed = summed + thin
                speed = coef[at]
                gradient = summed / speed
                total[at] = gradient
                sample[at] = (
                    speed
                    + step_eta * (prior_prec * (prior_centre - speed) - gradient)
                    + math.sqrt(2.0 * step_eta) * noise[at]
                )


def run_final(ours, theirs, thin_ours, thin_theirs, coef, noise):
    blocks = 128 // THIN
    part = pl.BlockSpec((coef.shape[0] // blocks,) + coef.shape[1:], lambda step: (step, 0, 0))
    thin = whole(thin_ours.shape)
    field = jax.ShapeDtypeStruct(coef.shape, jnp.float32)
    return pl.pallas_call(
        final_kernel,
        grid=(blocks,),
        in_specs=[part, part, thin, thin, part, part],
        out_specs=[part, part],
        out_shape=[field, field],
        compiler_params=pltpu.CompilerParams(vmem_limit_bytes=VMEM_LIMIT),
    )(ours, theirs, thin_ours, thin_theirs, coef, noise)


def receivers(observed, recv_tile, recv_cell, cell_count):
    tile_count = lax.axis_size(("gx", "gy"))
    highest = lax.Precision.HIGHEST
    tile_of = recv_tile[:, 0]
    per_tile = max(2, 2 * observed.shape[1] // tile_count)
    slot_count = tile_count * per_tile
    owner_hot = (tile_of[:, None] == jnp.arange(tile_count, dtype=jnp.int32)[None, :]).astype(
        jnp.int32
    )
    before = jnp.cumsum(owner_hot, 0) - owner_hot
    slot_of = tile_of * per_tile + jnp.sum(before * owner_hot, 1)
    routing = (slot_of[None, :] == jnp.arange(slot_count, dtype=jnp.int32)[:, None]).astype(
        jnp.float32
    )
    traces = jnp.pad(-observed[0][:, ::-1], ((0, 0), (DEPTH, 128 - DEPTH - STEPS)))
    marks = (recv_cell + 1).astype(jnp.float32)[:, None]
    lanes = jnp.arange(128, dtype=jnp.int32)[None, :]
    outgoing = jnp.dot(
        routing,
        jnp.where(lanes == MARK, marks, traces),
        precision=highest,
        preferred_element_type=jnp.float32,
    )
    arrived = lax.all_to_all(
        outgoing.reshape(tile_count, per_tile, 128),
        ("gx", "gy"),
        split_axis=0,
        concat_axis=0,
        tiled=True,
    ).reshape(slot_count, 128)
    cells = arrived[:, MARK].astype(jnp.int32) - 1
    picker = (jnp.arange(cell_count, dtype=jnp.int32)[:, None] == cells[None, :]).astype(
        jnp.float32
    )
    seen = jnp.dot(
        picker,
        jnp.where(lanes < THIN, arrived, 0.0),
        precision=highest,
        preferred_element_type=jnp.float32,
    )
    return jnp.sum(picker, 1, keepdims=True), seen


def local(
    coef, wave_now, wave_prev, adjoint_next, adjoint_after, noise, observed, recv_tile, recv_cell
):
    rows, cols, depth = coef.shape
    odd_x, odd_y = lax.axis_index("gx") % 2, lax.axis_index("gy") % 2
    parity = jnp.stack([odd_x, odd_y]).astype(jnp.int32)
    after = lambda value, *earlier: lax.optimization_barrier((value, earlier))[0]

    fields = [wave_now[0], wave_prev[0], coef, adjoint_next[0], adjoint_after[0]]
    sends = strips(parity, fields, 0, K, limit=FIRST_VMEM_LIMIT)
    halos = swap("gx", *sends)
    early = after(parity, sends)
    sends_y = strips(early, fields, 1, K)
    halos += swap("gy", *sends_y)
    counts, seen = receivers(after(observed, sends_y), recv_tile, recv_cell, rows * cols)
    speeds = jnp.pad(coef[:, :, :THIN], ((0, 0), (0, 0), (THIN, 128 - 2 * THIN)))
    sends = strips(after(parity, counts, seen, speeds), [], 1, K, halos[:2])
    halos += swap("gy", *sends)

    wave = (after(parity, sends), *fields[:3], halos, halos)
    now, then, *sends, laps_early, surface = run_block(*wave, False)
    wave_mid = swap("gx", *sends)
    sends_y = strips(after(parity, sends), [now, then], 1, K)
    wave_mid += swap("gy", *sends_y)
    adjoint = (after(parity, sends_y), *fields[3:], coef, halos, halos)
    later, latest, *late_sends, ahead = run_block(*adjoint, True, first_part=3)
    sends = strips(after(parity, late_sends), [], 1, K, wave_mid[:2])
    wave_mid += swap("gy", *sends)
    adjoint_mid = swap("gx", *after(late_sends, sends))
    wave = (parity, now, then, coef, wave_mid, halos)
    gradient, laps_late, surface = run_block(*wave, False, (ahead, surface))
    thin = counts * surface.reshape(rows * cols, 128) + seen
    thin = thin.reshape(rows, cols, 128) + speeds
    sends = strips(after(parity, surface), [later, latest], 1, K, adjoint_mid)
    adjoint_mid += swap("gy", *sends)
    sends = strips(parity, [thin], 0, STEPS)
    thin_halos = swap("gx", *sends)
    sends = strips(parity, [thin], 1, STEPS, thin_halos)
    thin_halos += swap("gy", *sends)
    adjoint = (after(parity, sends), later, latest, coef, adjoint_mid, halos)
    (gradient,) = run_block(*adjoint, True, (laps_early, gradient))
    shots = pairs(lax.axis_size("shot"), False)
    other = lax.ppermute(after(gradient, thin_halos), "shot", shots)
    thin_gradient = run_thin(parity, thin, thin_halos, laps_early, laps_late)
    thin_other = lax.ppermute(thin_gradient, "shot", shots)
    return tuple(run_final(gradient, other, thin_gradient, thin_other, coef, noise))


def solution(mesh):
    return jax.shard_map(
        local,
        mesh=mesh,
        in_specs=(
            P("gx", "gy", None),
            P("shot", "gx", "gy", None),
            P("shot", "gx", "gy", None),
            P("shot", "gx", "gy", None),
            P("shot", "gx", "gy", None),
            P("gx", "gy", None),
            P("shot", ("gx", "gy"), None),
            P(("gx", "gy"), None),
            P(("gx", "gy")),
        ),
        out_specs=(P("gx", "gy", None), P("gx", "gy", None)),
        check_vma=False,
    )
```
